128 devices in a mesh: row: 16 (over z, y), col: 8 (over x, core).
Axes of the slice: x: 4, y: 4, z: 4, core: 2. Of those that a mesh axis runs over, the one named last changes fastest.
Arguments:
- sample: float32 [2, 8192, 8192], P(None, 'row', 'col'), may hold values from -6 to 6
- probe_field: float32 [2, 256, 256], replicated, may hold values from -6 to 6
- patterns: float32 [2048, 256, 256], P(('row', 'col')), may hold values from 1 to 16
- positions: int32 [2048, 2], P(('row', 'col')), may hold values from 0 to 8191, as said below
- counts: int32 [128], replicated, may hold values from 1 to 16, as said below
Outputs:
- object_grad: float32 [2, 8192, 8192], P(None, 'row', 'col')
- probe_grad: float32 [2, 256, 256], replicated
- mean_misfit: float32 [], replicated
The draws below stay inside these ranges and needn't reach their ends.
Inputs may be any that keep to these rules, and one draw needn't show every extreme that they name: `positions`: slot s lies in the block of slots of tile s // 16 (tiles in row-major order over the object's 16 x 8 tiles), and its top-left pixel lies inside that tile. `counts`: some tile has all 16 slots live.
All inputs are finite; a program needn't handle non-finite values.
Results may differ from the reference program's by a relative error of at most 0.0003.
Values sent between devices are 32-bit elements; how exact they have to be, the bound alone decides.
A program may use at most 128 MiB of HBM per device.

```python
import math
import jax
import jax.numpy as jnp
from jax import lax

M = 256
TR = 512
TC = 1024
CAP = 16
NR = 8192
NC = 8192
SLOTS = 2048
N_ROW = 16
N_COL = 8


def draw_positions(key, part):
    key = jax.random.fold_in(key, 11)
    key_rows, key_cols = jax.random.split(key)
    slot_ids = jnp.arange(SLOTS, dtype=jnp.int32)
    tile_ids = slot_ids // CAP
    tile_row = tile_ids // N_COL
    tile_col = tile_ids % N_COL
    rows = jax.random.randint(key_rows, (SLOTS,), 0, TR, dtype=jnp.int32) + tile_row * TR
    cols = jax.random.randint(key_cols, (SLOTS,), 0, TC, dtype=jnp.int32) + tile_col * TC
    rows = jnp.where(slot_ids == 0, 0, rows)
    cols = jnp.where(slot_ids == 0, 0, cols)
    rows = jnp.where(slot_ids == SLOTS - 1, NR - 1, rows)
    cols = jnp.where(slot_ids == SLOTS - 1, NC - 1, cols)
    return jnp.stack([rows, cols], axis=1).astype(jnp.int32)


def draw_counts(key, part):
    key = jax.random.fold_in(key, 23)
    key_count, key_full = jax.random.split(key)
    tiles = N_ROW * N_COL
    values = jax.random.randint(key_count, (tiles,), 1, CAP + 1, dtype=jnp.int32)
    fullest = jax.random.randint(key_full, (), 0, tiles, dtype=jnp.int32)
    values = jnp.where(jnp.arange(tiles, dtype=jnp.int32) == fullest, CAP, values)
    return values.astype(jnp.int32)


def level_of(own_key, dims, cuts, smallest, largest):
    gain = 1.0
    for position, parts in cuts:
        steps = jax.random.uniform(jax.random.fold_in(jax.random.fold_in(own_key, 6), position), (parts,), jnp.float32, smallest / len(cuts), largest / len(cuts))
        gain = gain * jnp.repeat(jnp.exp(steps), dims[position] // parts).reshape((-1,) + (1,) * (len(dims) - 1 - position))
    return gain


def scatter_about(rng, dims, width, limit, shards=(), kind=jnp.bfloat16):
    values = jax.random.normal(rng, dims, jnp.float32) * width
    if len(shards) > 0:
        values = level_of(rng, dims, shards, -0.22, 0.18) * values
    return jnp.clip(values, min=-limit, max=limit).astype(kind)


def setup_inputs(seed: int = 0) -> dict:
    keys = jax.random.split(jax.random.key(seed), 6)
    sample = scatter_about(keys[0], (2, NR, NC), 1.0, 6.0, ((1, 16), (2, 8)), jnp.float32)
    probe_field = scatter_about(keys[1], (2, M, M), 1.0, 6.0, (), jnp.float32)
    patterns = jnp.clip(jnp.exp(math.log(16.0) - 2.7725887 * jax.random.uniform(keys[2], (SLOTS, M, M), jnp.float32) ** level_of(keys[2], (SLOTS, M, M), ((0, 128),), -0.2, 0.2)), 1.0, 16.0)
    positions = draw_positions(jax.random.fold_in(keys[5], 71), 0)
    counts = draw_counts(jax.random.fold_in(keys[5], 71), 0)
    return dict(sample=sample, probe_field=probe_field, patterns=patterns, positions=positions, counts=counts)


def reference(sample, probe_field, patterns, positions, counts):
    slot_ids = jnp.arange(SLOTS, dtype=jnp.int32)
    weights = (slot_ids % CAP < counts[slot_ids // CAP]).astype(jnp.float32)
    visits = jnp.sum(counts).astype(jnp.float32)
    measured = jnp.sum(jnp.sum(patterns, axis=(1, 2)) * weights)
    mean_level = measured / (M * M * visits)
    coeff = 4.0 / (mean_level * mean_level)
    padded = jnp.pad(sample, ((0, 0), (0, M), (0, M)))
    probe_re = probe_field[0]
    probe_im = probe_field[1]

    def visit(carry, item):
        grad_field, probe_acc, misfit = carry
        corner, pattern, weight = item
        start = (jnp.int32(0), corner[0].astype(jnp.int32), corner[1].astype(jnp.int32))
        patch = lax.dynamic_slice(padded, start, (2, M, M))
        exit_wave = lax.complex(probe_re * patch[0] - probe_im * patch[1], probe_re * patch[1] + probe_im * patch[0])
        far_field = jnp.fft.fft2(exit_wave, norm="ortho")
        intensity = far_field.real * far_field.real + far_field.imag * far_field.imag
        resid = (intensity - pattern) * weight
        back = jnp.fft.ifft2(resid * far_field, norm="ortho")
        back_re = back.real
        back_im = back.imag
        update = jnp.stack([probe_re * back_re + probe_im * back_im, probe_re * back_im - probe_im * back_re])
        current = lax.dynamic_slice(grad_field, start, (2, M, M))
        grad_field = lax.dynamic_update_slice(grad_field, current + update, start)
        probe_acc = probe_acc + jnp.stack([patch[0] * back_re + patch[1] * back_im, patch[0] * back_im - patch[1] * back_re])
        misfit = misfit + jnp.sum(resid * resid)
        return (grad_field, probe_acc, misfit), None

    init = (jnp.zeros_like(padded), jnp.zeros((2, M, M), jnp.float32), jnp.zeros((), jnp.float32))
    (grad_field, probe_acc, misfit), _ = lax.scan(visit, init, (positions, patterns, weights))
    object_grad = coeff * grad_field[:, :NR, :NC]
    probe_grad = (coeff / visits) * probe_acc
    mean_misfit = misfit / (mean_level * mean_level * M * M * visits)
    return object_grad, probe_grad, mean_misfit
```

```python
import math

import jax
import jax.numpy as jnp
import numpy as np
from jax import lax
from jax.experimental import pallas as pl
from jax.experimental.pallas import tpu as pltpu
from jax.sharding import PartitionSpec as P

F32 = jnp.float32
BF16 = jnp.bfloat16
M = 256
H = 128
CAP = 16


def split_table(table):
    high = table.astype(np.float32).astype(jnp.bfloat16)
    low = (table - high.astype(np.float64)).astype(np.float32).astype(jnp.bfloat16)
    return high, low


def dft_tables():
    n = np.arange(H)[:, None]
    m = np.arange(H)[None, :]
    right, left = [], []
    for sign in (-1.0, 1.0):
        for odd in (0, 1):
            if sign < 0:
                angle = 2 * math.pi * (n * (2 * m + odd) % M) / M
            else:
                angle = 2 * math.pi * ((2 * n + odd) * m % M) / M
            re, im = np.cos(angle) / 16.0, sign * np.sin(angle) / 16.0
            high, low = split_table(np.block([[re, im], [-im, re]]))
            right.append(np.concatenate([high, high, low], axis=0))
            re, im = re.T, im.T
            high, low = split_table(np.block([[re, -im], [im, re]]))
            left.append(np.concatenate([high, low, high], axis=1))
    order = np.zeros((M, M), np.float32)
    k = np.arange(M)
    order[k, k // 2 + H * (k % 2)] = 1.0
    order = np.concatenate([order, order], axis=0).astype(jnp.bfloat16)
    return np.stack(right), np.stack(left), order


def split(value):
    high = value.astype(BF16)
    return high, (value - high.astype(F32)).astype(BF16)


def dot(a, b):
    return jnp.dot(a, b, preferred_element_type=F32)


def right_dot(value, table):
    high, low = split(value)
    return dot(jnp.concatenate([high, low, high], axis=1), table)


def left_dot(table, value):
    high, low = split(value)
    return dot(table, jnp.concatenate([high, high, low], axis=0))


def lanes(a, b):
    return jnp.concatenate([a, b], axis=1)


def rows(a, b):
    return jnp.concatenate([a, b], axis=0)


def one_window(top, j0, dc, ext, acc, pat, probe, right, left, order, pacc, mis, rolled, patch):
    mask = lax.broadcasted_iota(jnp.int32, (M, H), 1) >= dc

    def turned(a, b, shift, keep):
        a, b = pltpu.roll(a, shift, 1), pltpu.roll(b, shift, 1)
        return jnp.where(keep, a, b), jnp.where(keep, b, a)

    for p in range(2):
        a, b = turned(probe[p, :, :H], probe[p, :, H:], dc, mask)
        rolled[p, :, :H] = a
        rolled[p, :, H:] = b
        at = pl.ds(top, M)
        patch[p, :, :H] = jnp.where(mask, ext[p, j0, at, :], ext[p, j0 + 2, at, :])
        patch[p, :, H:] = ext[p, j0 + 1, at, :]
    wave_re = rolled[0] * patch[0] - rolled[1] * patch[1]
    wave_im = rolled[0] * patch[1] + rolled[1] * patch[0]
    sum_re, sum_im = wave_re[:, :H] + wave_re[:, H:], wave_im[:, :H] + wave_im[:, H:]
    dif_re, dif_im = wave_re[:, :H] - wave_re[:, H:], wave_im[:, :H] - wave_im[:, H:]
    even = right_dot(lanes(sum_re, sum_im), right[0])
    odd = right_dot(lanes(dif_re, dif_im), right[1])
    even_s, even_d = even[:H] + even[H:], even[:H] - even[H:]
    odd_s, odd_d = odd[:H] + odd[H:], odd[:H] - odd[H:]
    back = []
    for parity, (e, o) in enumerate(((even_s, odd_s), (even_d, odd_d))):
        far = left_dot(left[parity], rows(lanes(e[:, :H], o[:, :H]), lanes(e[:, H:], o[:, H:])))
        far_re, far_im = far[:H], far[H:]
        every = pl.ds(parity, H, 2)
        high, low = split(lanes(pat[0, every, :], pat[1, every, :]))
        measured = dot(lanes(high, low), order[...])
        resid = far_re * far_re + far_im * far_im - measured
        mis[...] += jnp.sum((resid * resid).reshape(16, 8, M), axis=0)
        back.append(left_dot(left[2 + parity], rows(resid * far_re, resid * far_im)))
    half_s, half_d = back[0] + back[1], back[0] - back[1]
    mid_re = rows(half_s[:H], half_d[:H])
    mid_im = rows(half_s[H:], half_d[H:])
    even = right_dot(lanes(mid_re[:, :H], mid_im[:, :H]), right[2])
    odd = right_dot(lanes(mid_re[:, H:], mid_im[:, H:]), right[3])
    first, second = even + odd, even - odd
    back_re = lanes(first[:, :H], second[:, :H])
    back_im = lanes(first[:, H:], second[:, H:])
    unmask = lax.broadcasted_iota(jnp.int32, (M, H), 1) < H - dc
    undo = lax.rem(H - dc, H)
    for p in range(2):
        if p == 0:
            update = rolled[0] * back_re + rolled[1] * back_im
            grad = patch[0] * back_re + patch[1] * back_im
        else:
            update = rolled[0] * back_im - rolled[1] * back_re
            grad = patch[0] * back_im - patch[1] * back_re
        acc[p, j0, at, :] += jnp.where(mask, update[:, :H], 0.0)
        acc[p, j0 + 2, at, :] += jnp.where(mask, 0.0, update[:, :H])
        acc[p, j0 + 1, at, :] += update[:, H:]
        a, b = turned(grad[:, :H], grad[:, H:], undo, unmask)
        pacc[p, :, :H] += a
        pacc[p, :, H:] += b


def windows_kernel(plan, *refs):
    names = plan["names"]
    at = dict(zip(names, refs))
    ext, acc = at["ext"], at["acc"]
    pos, count = at["pos"], at["count"]
    n_pieces, n_carry = len(plan["pieces"]), len(plan["carry"])
    nblk = plan["nblk"]

    def here(s):
        o, c = pos[s, 0], pos[s, 1]
        return (s < count[0]) & plan["cond"](o, c)

    copies = []

    def begin(src, dst):
        copy = pltpu.make_async_copy(src, dst, at["sems"].at[len(copies)])
        copy.start()
        copies.append(copy)

    def pattern_copies(s):
        return [
            pltpu.make_async_copy(at["patterns"].at[s, :, pl.ds(k * H, H)], at["pat"].at[s, k], at["pat_sems"].at[s, k])
            for k in range(2)
        ]

    for ref, (r0, c0, nr, nc, dr, db) in zip(at["pieces"], plan["pieces"]):
        for k in range(nc // H):
            begin(ref.at[:, pl.ds(r0, nr), pl.ds(c0 + k * H, H)], ext.at[:, db + k, pl.ds(dr, nr), :])
    for ref, (r0, nr, nc, dr, db) in zip(at["carry"], plan["carry"]):
        for k in range(nc // H):
            begin(ref.at[:, pl.ds(r0, nr), pl.ds(k * H, H)], acc.at[:, db + k, pl.ds(dr, nr), :])

    @pl.loop(0, CAP)
    def _(s):
        @pl.when(here(s))
        def _():
            for copy in pattern_copies(s):
                copy.start()

    for b in range(nblk):
        kept = plan["carried"].get(b, 0)
        if kept:
            acc[:, b, :-kept] = jnp.zeros_like(acc[:, b, :-kept])
        else:
            acc[:, b] = jnp.zeros_like(acc[:, b])
    at["pacc"][...] = at["pacc_in"][...]
    at["mis"][...] = at["mis_in"][...]
    for copy in copies:
        copy.wait()

    @pl.loop(0, CAP)
    def _(s):
        @pl.when(here(s))
        def _():
            for copy in pattern_copies(s):
                copy.wait()
            o, c = pos[s, 0] - plan["row0"], pos[s, 1] - plan["col0"]
            one_window(o, c // H, c % H, ext, acc, at["pat"].at[s], at["probe"], at["right"], at["left"],
                       at["order"], at["pacc"], at["mis"], at["rolled"], at["patch"])

    ends = []
    for ref, (r0, nr, nc, db) in zip(at["outs"], plan["outs"]):
        for k in range(nc // H):
            copy = pltpu.make_async_copy(acc.at[:, db + k, pl.ds(r0, nr), :], ref.at[:, :, pl.ds(k * H, H)],
                                         at["sems"].at[len(copies) + len(ends)])
            copy.start()
            ends.append(copy)
    for copy in ends:
        copy.wait()


def windows(name, pos, count, patterns, probe, tables, pacc, mis, pieces, carry, outs, nblk, nrows, row0, col0, cond, cost=8):
    right, left, order = tables
    vm = pl.BlockSpec(memory_space=pltpu.VMEM)
    sm = pl.BlockSpec(memory_space=pltpu.SMEM)
    hbm = pl.BlockSpec(memory_space=pl.ANY)
    plan = dict(
        pieces=[p[1:] for p in pieces], carry=[c[1:] for c in carry], outs=outs, nblk=nblk, row0=row0, col0=col0, cond=cond,
        carried={c[5] + k: c[2] for c in carry for k in range(c[3] // H)},
    )
    n_p, n_c, n_o = len(pieces), len(carry), len(outs)
    n_sems = sum(p[4] // H for p in pieces) + sum(c[3] // H for c in carry) + sum(o[2] // H for o in outs)

    def kernel(*refs):
        it = iter(refs)
        take = lambda n: [next(it) for _ in range(n)]
        at = {}
        at["pos"], at["count"], at["patterns"], at["probe"], at["right"], at["left"], at["order"], at["pacc_in"], at["mis_in"] = take(9)
        at["pieces"], at["carry"], at["outs"] = take(n_p), take(n_c), take(n_o)
        at["pacc"], at["mis"] = take(2)
        at["ext"], at["acc"], at["pat"], at["rolled"], at["patch"], at["sems"], at["pat_sems"] = take(7)
        windows_kernel(dict(plan, names=list(at)), *at.values())

    out = pl.pallas_call(
        kernel,
        name=name,
        out_shape=[jax.ShapeDtypeStruct((2, nr, nc), F32) for _, nr, nc, _ in outs]
        + [jax.ShapeDtypeStruct((2, M, M), F32), jax.ShapeDtypeStruct((8, M), F32)],
        in_specs=[sm, sm, hbm, vm, vm, vm, vm, vm, vm] + [hbm] * (n_p + n_c),
        out_specs=[hbm] * n_o + [vm, vm],
        scratch_shapes=[
            pltpu.VMEM((2, nblk, nrows, H), F32),
            pltpu.VMEM((2, nblk, nrows, H), F32),
            pltpu.VMEM((CAP, 2, M, H), F32),
            pltpu.VMEM((2, M, M), F32),
            pltpu.VMEM((2, M, M), F32),
            pltpu.SemaphoreType.DMA((n_sems,)),
            pltpu.SemaphoreType.DMA((CAP, 2)),
        ],
        compiler_params=pltpu.CompilerParams(vmem_limit_bytes=48 << 20),
        cost_estimate=pl.CostEstimate(flops=cost * 26 * 2 * M**3, bytes_accessed=8 << 20, transcendentals=0),
    )(pos, count, patterns, probe, right, left, order, pacc, mis, *[p[0] for p in pieces], *[c[0] for c in carry])
    return out[:n_o], out[n_o], out[n_o + 1]


MESH = pl.DeviceIdType.MESH
NROW, NCOL = 16, 8


def total_kernel(pacc, scal, out, tot, mine1, got1, mine2, got2, part, wide, s1, r1, s2, r2, s3, r3, s4, r4):
    row, col = lax.axis_index("row"), lax.axis_index("col")

    def col_peer(k):
        return row, lax.rem(col + k, NCOL)

    def row_peer(k):
        return lax.rem(row + k, NROW), col

    barrier = pltpu.get_barrier_semaphore()
    for k in range(1, NCOL):
        pl.semaphore_signal(barrier, inc=1, device_id=col_peer(k), device_id_type=MESH)
    for k in range(1, NROW):
        pl.semaphore_signal(barrier, inc=1, device_id=row_peer(k), device_id_type=MESH)
    for p in range(2):
        for b in range(2):
            for h in range(2):
                piece = 4 * p + 2 * b + h
                mine1[piece, :H] = pacc[p, h * H : (h + 1) * H, b * H : (b + 1) * H]
                mine1[piece, H:] = scal[...]
    pl.semaphore_wait(barrier, NCOL + NROW - 2)

    def send(src, dst, ss, rs, peer):
        copy = pltpu.make_async_remote_copy(src, dst, ss, rs, device_id=peer, device_id_type=MESH)
        copy.start()
        return copy

    copies = [
        send(mine1.at[lax.rem(col + k, NCOL)], got1.at[k - 1], s1.at[k - 1], r1.at[k - 1], col_peer(k))
        for k in range(1, NCOL)
    ]
    for copy in copies:
        copy.wait()
    total = mine1[col]
    for k in range(NCOL - 1):
        total = total + got1[k]
    for k in range(NROW):
        mine2[k, :8] = total[8 * k : 8 * k + 8]
        mine2[k, 8:] = total[H:]
    copies = [
        send(mine2.at[lax.rem(row + k, NROW)], got2.at[k - 1], s2.at[k - 1], r2.at[k - 1], row_peer(k))
        for k in range(1, NROW)
    ]
    for copy in copies:
        copy.wait()
    total = mine2[row]
    for k in range(NROW - 1):
        total = total + got2[k]
    tot[...] = total[8:]
    part[row] = total[:8]
    copies = [send(part.at[row], part.at[row], s3.at[k - 1], r3.at[k - 1], row_peer(k)) for k in range(1, NROW)]
    for copy in copies:
        copy.wait()
    copies = [send(part, wide.at[col], s4.at[k - 1], r4.at[k - 1], col_peer(k)) for k in range(1, NCOL)]
    wide[col] = part[...]
    for copy in copies:
        copy.wait()
    for p in range(2):
        for b in range(2):
            for h in range(2):
                out[p, h * H : (h + 1) * H, b * H : (b + 1) * H] = wide[4 * p + 2 * b + h].reshape(H, H)


def total_over_devices(pacc, scal):
    vm = pl.BlockSpec(memory_space=pltpu.VMEM)
    sems = [pltpu.SemaphoreType.DMA((n,)) for n in (NCOL - 1, NCOL - 1, NROW - 1, NROW - 1, NROW - 1, NROW - 1, NCOL - 1, NCOL - 1)]
    return pl.pallas_call(
        total_kernel,
        name="total_over_devices",
        out_shape=[jax.ShapeDtypeStruct((2, M, M), F32), jax.ShapeDtypeStruct((8, H), F32)],
        in_specs=[vm, vm],
        out_specs=[vm, vm],
        scratch_shapes=[
            pltpu.VMEM((NCOL, H + 8, H), F32),
            pltpu.VMEM((NCOL - 1, H + 8, H), F32),
            pltpu.VMEM((NROW, 16, H), F32),
            pltpu.VMEM((NROW - 1, 16, H), F32),
            pltpu.VMEM((NROW, 8, H), F32),
            pltpu.VMEM((NCOL, NROW, 8, H), F32),
        ]
        + sems,
        compiler_params=pltpu.CompilerParams(collective_id=0, has_side_effects=True),
        cost_estimate=pl.CostEstimate(flops=12 * 10**9, bytes_accessed=8 << 20, transcendentals=0),
    )(pacc, scal)


def passed_along(value, axis, steps):
    count = lax.axis_size(axis)
    first, last = (max(0, -steps), min(count, count - steps))
    return lax.ppermute(value, axis, [(source, source + steps) for source in range(first, last)])


def body(sample, probe, patterns, positions, counts):
    tile_rows, tile_cols = sample.shape[1:]
    row_at, col_at = lax.axis_index("row"), lax.axis_index("col")
    own = counts[row_at * NCOL + col_at]
    pos = positions - jnp.stack([row_at * tile_rows, col_at * tile_cols])[None, :]
    count = own.reshape(1)
    visits = jnp.sum(counts).astype(F32)
    low = [None] * 4
    low[0] = passed_along(sample[:, :M, :M], "row", -1)
    right = passed_along(sample[:, :, :M], "col", -1)
    for k in (3, 2, 1):
        low[k] = passed_along(sample[:, :M, k * M : (k + 1) * M], "row", -1)
    corner = passed_along(low[0], "col", -1)
    tables = tuple(jnp.asarray(t) for t in dft_tables())
    live = (jnp.arange(CAP, dtype=jnp.int32) < own).astype(F32)
    measured = jnp.sum(jnp.sum(patterns, axis=(1, 2)) * live)

    args = (pos, count, patterns, probe, tables)
    (inner,), pacc, mis = windows(
        "windows_inside", *args, jnp.zeros((2, M, M), F32), jnp.zeros((8, M), F32),
        [(sample, 0, 0, 512, 1024, 0, 0)], [], [(0, 512, 1024, 0)],
        8, 512, 0, 0, lambda o, c: (o <= M) & (c < 768), cost=16,
    )
    (own4, edge, part3), pacc, mis = windows(
        "windows_right", *args, pacc, mis,
        [(sample, 0, 768, 512, 256, 0, 0), (right, 0, 0, 512, 256, 0, 2), (low[3], 0, 0, M, M, 512, 0), (corner, 0, 0, M, M, 512, 2)],
        [], [(0, 512, M, 0), (0, 768, M, 2), (512, M, M, 0)],
        4, 768, 0, 768, lambda o, c: c >= 768, cost=6,
    )
    came_right = passed_along(edge, "col", 1)
    (own3, halo3, part2), pacc, mis = windows(
        "windows_third", *args, pacc, mis,
        [(sample, 256, 512, 256, 512, 0, 0), (low[2], 0, 0, M, M, 256, 0), (low[3], 0, 0, M, M, 256, 2)],
        [(part3, 0, M, M, 256, 2)], [(0, M, 512, 0), (256, M, M, 2), (256, M, M, 0)],
        4, 512, 256, 512, lambda o, c: (o > M) & (c >= 512) & (c < 768), cost=4,
    )
    down3 = passed_along(halo3, "row", 1)
    (own12, halo12), pacc, mis = windows(
        "windows_left", *args, pacc, mis,
        [(sample, 256, 0, 256, 768, 0, 0), (low[0], 0, 0, M, M, 256, 0), (low[1], 0, 0, M, M, 256, 2), (low[2], 0, 0, M, M, 256, 4)],
        [(part2, 0, M, M, 256, 4), (came_right, 512, M, M, 256, 0)], [(0, M, 768, 0), (256, M, 768, 0)],
        6, 512, 256, 0, lambda o, c: (o > M) & (c < 512), cost=6,
    )
    down12 = passed_along(halo12, "row", 1)
    lane = lax.broadcasted_iota(jnp.int32, (8, H), 1)
    first = lax.broadcasted_iota(jnp.int32, (8, H), 0) == 0
    scal = jnp.where(first & (lane == 0), measured, jnp.where(first & (lane == 1), jnp.sum(mis), 0.0))
    probe_sum, totals = total_over_devices(pacc, scal)
    mean_level = totals[0, 0] / (M * M * visits)
    coeff = 4.0 / (mean_level * mean_level)
    summed = inner
    summed = summed.at[:, :, 768:].add(own4)
    summed = summed.at[:, M:, 512:].add(own3)
    summed = summed.at[:, M:, :768].add(own12)
    summed = summed.at[:, :, :M].add(came_right[:, :512])
    summed = summed.at[:, :M, 768:].add(down3)
    summed = summed.at[:, :M, :768].add(down12)
    mean_misfit = totals[0, 1] / (mean_level * mean_level * M * M * visits)
    return summed * coeff, probe_sum * (coeff / visits), mean_misfit


def solution(mesh):
    in_specs = (
        P(None, "row", "col"),
        P(),
        P(("row", "col"), None, None),
        P(("row", "col"), None),
        P(),
    )
    out_specs = (P(None, "row", "col"), P(), P())
    return jax.shard_map(body, mesh=mesh, in_specs=in_specs, out_specs=out_specs, check_vma=False)
```

```python
import math

import jax
import jax.numpy as jnp
import numpy as np
from jax import lax
from jax.experimental import pallas as pl
from jax.experimental.pallas import tpu as pltpu
from jax.sharding import PartitionSpec as P

F32 = jnp.float32
BF16 = jnp.bfloat16
M = 256
H = 128
CAP = 16
SIDE = 2
LAG = 0


def split_table(table):
    high = table.astype(np.float32).astype(jnp.bfloat16)
    low = (table - high.astype(np.float64)).astype(np.float32).astype(jnp.bfloat16)
    return high, low


def dft_tables():
    n = np.arange(H)[:, None]
    m = np.arange(H)[None, :]
    right, left = [], []
    for sign in (-1.0, 1.0):
        for odd in (0, 1):
            if sign < 0:
                angle = 2 * math.pi * (n * (2 * m + odd) % M) / M
            else:
                angle = 2 * math.pi * ((2 * n + odd) * m % M) / M
            re, im = np.cos(angle) / 16.0, sign * np.sin(angle) / 16.0
            high, low = split_table(np.block([[re, im], [-im, re]]))
            right.append(np.concatenate([high, high, low], axis=0))
            re, im = re.T, im.T
            high, low = split_table(np.block([[re, -im], [im, re]]))
            left.append(np.concatenate([high, low, high], axis=1))
    order = np.zeros((M, M), np.float32)
    k = np.arange(M)
    order[k, k // 2 + H * (k % 2)] = 1.0
    order = np.concatenate([order, order], axis=0).astype(jnp.bfloat16)
    return np.stack(right), np.stack(left), order


def split(value):
    high = value.astype(BF16)
    return high, (value - high.astype(F32)).astype(BF16)


def dot(a, b):
    return jnp.dot(a, b, preferred_element_type=F32)


def right_dot(value, table):
    high, low = split(value)
    return dot(jnp.concatenate([high, low, high], axis=1), table)


def left_dot(table, value):
    high, low = split(value)
    return dot(table, jnp.concatenate([high, high, low], axis=0))


def lanes(a, b):
    return jnp.concatenate([a, b], axis=1)


def rows(*parts):
    return jnp.concatenate(parts, axis=0)


def one_window(spot, ext, acc, probe, right, left, order, pacc, stats, rolled, patch):
    top, j0, dc, pat = spot
    lane = lax.broadcasted_iota(jnp.int32, (M, H), 1)
    mask = lane >= dc
    at = pl.ds(top, M)

    def turned(a, b, shift, keep):
        a, b = pltpu.roll(a, shift, 1), pltpu.roll(b, shift, 1)
        return jnp.where(keep, a, b), jnp.where(keep, b, a)

    for p in range(2):
        a, b = turned(probe[p, :, :H], probe[p, :, H:], dc, mask)
        rolled[p, :, :H] = a
        rolled[p, :, H:] = b
        patch[p, :, :H] = jnp.where(mask, ext[p, j0, at, :], ext[p, j0 + 2, at, :])
        patch[p, :, H:] = ext[p, j0 + 1, at, :]
    wave_re = rolled[0] * patch[0] - rolled[1] * patch[1]
    wave_im = rolled[0] * patch[1] + rolled[1] * patch[0]
    sums = lanes(wave_re[:, :H] + wave_re[:, H:], wave_im[:, :H] + wave_im[:, H:])
    difs = lanes(wave_re[:, :H] - wave_re[:, H:], wave_im[:, :H] - wave_im[:, H:])
    yield
    even = right_dot(sums, right[0])
    odd = right_dot(difs, right[1])
    yield
    halves = ((even[:H] + even[H:], odd[:H] + odd[H:]), (even[:H] - even[H:], odd[:H] - odd[H:]))
    fars, levels = [], []
    for parity, (e, o) in enumerate(halves):
        fars.append(left_dot(left[parity], rows(lanes(e[:, :H], o[:, :H]), lanes(e[:, H:], o[:, H:]))))
        every = pl.ds(parity, H, 2)
        level = lanes(pat[0, every, :], pat[1, every, :])
        stats[8:] += jnp.sum(level.reshape(16, 8, M), axis=0)
        high, low = split(level)
        levels.append(dot(lanes(high, low), order[...]))
        yield
    back = []
    for parity, far in enumerate(fars):
        far_re, far_im = far[:H], far[H:]
        resid = far_re * far_re + far_im * far_im - levels[parity]
        stats[:8] += jnp.sum((resid * resid).reshape(16, 8, M), axis=0)
        back.append(left_dot(left[2 + parity], rows(resid * far_re, resid * far_im)))
        yield
    half_s, half_d = back[0] + back[1], back[0] - back[1]
    re, im = rows(half_s[:H], half_d[:H]), rows(half_s[H:], half_d[H:])
    even = right_dot(lanes(re[:, :H], im[:, :H]), right[2])
    odd = right_dot(lanes(re[:, H:], im[:, H:]), right[3])
    yield
    first, second = even + odd, even - odd
    back_re = lanes(first[:, :H], second[:, :H])
    back_im = lanes(first[:, H:], second[:, H:])
    unmask = lane < H - dc
    undo = lax.rem(H - dc, H)
    for p in range(2):
        if p == 0:
            update = rolled[0] * back_re + rolled[1] * back_im
            grad = patch[0] * back_re + patch[1] * back_im
        else:
            update = rolled[0] * back_im - rolled[1] * back_re
            grad = patch[0] * back_im - patch[1] * back_re
        acc[p, j0, at, :] += jnp.where(mask, update[:, :H], 0.0)
        acc[p, j0 + 2, at, :] += jnp.where(mask, 0.0, update[:, :H])
        acc[p, j0 + 1, at, :] += update[:, H:]
        a, b = turned(grad[:, :H], grad[:, H:], undo, unmask)
        pacc[p, :, :H] += a
        pacc[p, :, H:] += b
    yield


def some_windows(spots, ext, acc, probe, right, left, order, pacc, stats, rolled, patch):
    runs = [
        one_window(spot, ext, acc, probe, right, left, order, pacc, stats, rolled.at[w], patch.at[w])
        for w, spot in enumerate(spots)
    ]
    steps = 8
    for t in range(steps + LAG * (len(runs) - 1)):
        for w, run in enumerate(runs):
            if 0 <= t - LAG * w < steps:
                next(run)


def windows_kernel(plan, *refs):
    names = plan["names"]
    at = dict(zip(names, refs))
    ext, acc = at["ext"], at["acc"]
    pos, count = at["pos"], at["count"]
    n_pieces, n_carry = len(plan["pieces"]), len(plan["carry"])
    nblk = plan["nblk"]

    def here(s):
        o, c = pos[s, 0], pos[s, 1]
        return (s < count[0]) & plan["cond"](o, c)

    copies = []

    def begin(src, dst):
        copy = pltpu.make_async_copy(src, dst, at["sems"].at[len(copies)])
        copy.start()
        copies.append(copy)

    def pattern_copies(s):
        return [
            pltpu.make_async_copy(at["patterns"].at[s, :, pl.ds(k * H, H)], at["pat"].at[s, k], at["pat_sems"].at[s, k])
            for k in range(2)
        ]

    for ref, (r0, c0, nr, nc, dr, db) in zip(at["pieces"], plan["pieces"]):
        for k in range(nc // H):
            begin(ref.at[:, pl.ds(r0, nr), pl.ds(c0 + k * H, H)], ext.at[:, db + k, pl.ds(dr, nr), :])
    for ref, (r0, c0, nr, nc, dr, db) in zip(at["carry"], plan["carry"]):
        for k in range(nc // H):
            begin(ref.at[:, pl.ds(r0, nr), pl.ds(c0 + k * H, H)], acc.at[:, db + k, pl.ds(dr, nr), :])

    todo = at["todo"]

    def choose(s, n):
        todo[n] = s

        @pl.when(here(s))
        def _():
            for copy in pattern_copies(s):
                copy.start()

        return n + here(s).astype(jnp.int32)

    chosen = lax.fori_loop(0, CAP, choose, jnp.int32(0))
    for b, first, end in plan["zeros"]:
        acc[:, b, first:end] = jnp.zeros_like(acc[:, b, first:end])
    for name in ("pacc", "stats"):
        at[name][...] = at[name + "_in"][...] if plan["sums"] else jnp.zeros_like(at[name])
    for copy in copies:
        copy.wait()

    def spot(i):
        s = todo[i]
        for copy in pattern_copies(s):
            copy.wait()
        o, c = pos[s, 0] - plan["row0"], pos[s, 1] - plan["col0"]
        return o, c // H, c % H, at["pat"].at[s]

    def run(spots):
        some_windows(spots, ext, acc, at["probe"], at["right"], at["left"],
                     at["order"], at["pacc"], at["stats"], at["rolled"], at["patch"])

    @pl.loop(0, chosen // SIDE)
    def _(i):
        run([spot(SIDE * i + w) for w in range(SIDE)])

    @pl.loop(chosen // SIDE * SIDE, chosen)
    def _(i):
        run([spot(i)])

    ends = []
    for ref, (r0, nr, nc, db) in zip(at["outs"], plan["outs"]):
        for k in range(nc // H):
            copy = pltpu.make_async_copy(acc.at[:, db + k, pl.ds(r0, nr), :], ref.at[:, :, pl.ds(k * H, H)],
                                         at["sems"].at[len(copies) + len(ends)])
            copy.start()
            ends.append(copy)
    for copy in ends:
        copy.wait()


def windows(name, pos, count, patterns, probe, tables, sums, pieces, carry, outs, nblk, nrows, row0, col0, cond, cost=8):
    right, left, order = tables
    vm = pl.BlockSpec(memory_space=pltpu.VMEM)
    sm = pl.BlockSpec(memory_space=pltpu.SMEM)
    hbm = pl.BlockSpec(memory_space=pl.ANY)
    zeros = []
    for b in range(nblk):
        full = sorted((c[5], c[5] + c[3]) for c in carry if c[6] <= b < c[6] + c[4] // H)
        ends = [0] + [x for span in full for x in span] + [nrows]
        zeros += [(b, first, end) for first, end in zip(ends[::2], ends[1::2]) if end > first]
    plan = dict(
        pieces=[p[1:] for p in pieces], carry=[c[1:] for c in carry], outs=outs, nblk=nblk, row0=row0, col0=col0, cond=cond, sums=sums,
        zeros=zeros,
    )
    n_p, n_c, n_o = len(pieces), len(carry), len(outs)
    n_sems = sum(p[4] // H for p in pieces) + sum(c[4] // H for c in carry) + sum(o[2] // H for o in outs)

    def kernel(*refs):
        it = iter(refs)
        take = lambda n: [next(it) for _ in range(n)]
        at = {}
        at["pos"], at["count"], at["patterns"], at["probe"], at["right"], at["left"], at["order"] = take(7)
        at["pacc_in"], at["stats_in"] = take(2) if sums else (None, None)
        at["pieces"], at["carry"], at["outs"] = take(n_p), take(n_c), take(n_o)
        at["pacc"], at["stats"] = take(2)
        at["ext"], at["acc"], at["pat"], at["rolled"], at["patch"], at["sems"], at["pat_sems"], at["todo"] = take(8)
        windows_kernel(dict(plan, names=list(at)), *at.values())

    out = pl.pallas_call(
        kernel,
        name=name,
        out_shape=[jax.ShapeDtypeStruct((2, nr, nc), F32) for _, nr, nc, _ in outs]
        + [jax.ShapeDtypeStruct((2, M, M), F32), jax.ShapeDtypeStruct((16, M), F32)],
        in_specs=[sm, sm, hbm, vm, vm, vm, vm] + [vm] * len(sums) + [hbm] * (n_p + n_c),
        out_specs=[hbm] * n_o + [vm, vm],
        scratch_shapes=[
            pltpu.VMEM((2, nblk, nrows, H), F32),
            pltpu.VMEM((2, nblk, nrows, H), F32),
            pltpu.VMEM((CAP, 2, M, H), F32),
            pltpu.VMEM((SIDE, 2, M, M), F32),
            pltpu.VMEM((SIDE, 2, M, M), F32),
            pltpu.SemaphoreType.DMA((n_sems,)),
            pltpu.SemaphoreType.DMA((CAP, 2)),
            pltpu.SMEM((CAP,), jnp.int32),
        ],
        compiler_params=pltpu.CompilerParams(vmem_limit_bytes=48 << 20),
        cost_estimate=pl.CostEstimate(flops=cost, bytes_accessed=1 << 10, transcendentals=0),
    )(pos, count, patterns, probe, right, left, order, *sums, *[p[0] for p in pieces], *[c[0] for c in carry])
    return out[:n_o], tuple(out[n_o:])


MESH = pl.DeviceIdType.MESH
NROW, NCOL = 16, 8


def tail_kernel(visits, pacc, stats, halo, out, coeff, misfit, down, mine1, got1, mine2, got2, part, wide, s1, r1, s2, r2, s3, r3, s4, r4, s5, r5):
    row, col = lax.axis_index("row"), lax.axis_index("col")

    def col_peer(k):
        return row, lax.rem(col + k, NCOL)

    def row_peer(k):
        return lax.rem(row + k, NROW), col

    barrier = pltpu.get_barrier_semaphore()
    for k in range(1, NCOL):
        pl.semaphore_signal(barrier, inc=1, device_id=col_peer(k), device_id_type=MESH)
    for k in range(1, NROW):
        pl.semaphore_signal(barrier, inc=1, device_id=row_peer(k), device_id_type=MESH)
    for p in range(2):
        for b in range(2):
            for h in range(2):
                piece = 4 * p + 2 * b + h
                mine1[piece, :H] = pacc[p, h * H : (h + 1) * H, b * H : (b + 1) * H]
                mine1[piece, H:] = stats[:, :H] + stats[:, H:]
    pl.semaphore_wait(barrier, NCOL + NROW - 2)

    def send(src, dst, ss, rs, peer):
        copy = pltpu.make_async_remote_copy(src, dst, ss, rs, device_id=peer, device_id_type=MESH)
        copy.start()
        return copy

    pieces = []

    def send_pieces(n):
        for _ in range(n):
            k = len(pieces)
            cols = pl.ds(k * H, H)
            pieces.append(send(halo.at[:, :, cols], down.at[:, :, cols], s5.at[k], r5.at[k], row_peer(1)))

    copies = [
        send(mine1.at[lax.rem(col + k, NCOL)], got1.at[k - 1], s1.at[k - 1], r1.at[k - 1], col_peer(k))
        for k in range(1, NCOL)
    ]
    send_pieces(2)
    for copy in copies:
        copy.wait()
    total = mine1[col]
    for k in range(NCOL - 1):
        total = total + got1[k]
    for k in range(NROW):
        mine2[k, :8] = total[8 * k : 8 * k + 8]
        mine2[k, 8:] = total[H:]
    copies = [
        send(mine2.at[lax.rem(row + k, NROW)], got2.at[k - 1], s2.at[k - 1], r2.at[k - 1], row_peer(k))
        for k in range(1, NROW)
    ]
    send_pieces(1)
    for copy in copies:
        copy.wait()
    total = mine2[row]
    for k in range(NROW - 1):
        total = total + got2[k]
    pixels = M * M * visits[0]
    mean = jnp.full((8, H), jnp.sum(total[16:])) / pixels
    factor = 4.0 / (mean * mean)
    coeff[...] = factor
    misfit[...] = jnp.full((8, H), jnp.sum(total[8:16])) / (mean * mean * pixels)
    part[row] = total[:8] * (factor / visits[0])
    copies = [send(part.at[row], part.at[row], s3.at[k - 1], r3.at[k - 1], row_peer(k)) for k in range(1, NROW)]
    send_pieces(1)
    for copy in copies:
        copy.wait()
    copies = [send(part, wide.at[col], s4.at[k - 1], r4.at[k - 1], col_peer(k)) for k in range(1, NCOL)]
    send_pieces(2)
    wide[col] = part[...]
    for copy in copies + pieces:
        copy.wait()
    for p in range(2):
        for b in range(2):
            for h in range(2):
                out[p, h * H : (h + 1) * H, b * H : (b + 1) * H] = wide[4 * p + 2 * b + h].reshape(H, H)


def tail(visits, pacc, stats, halo):
    vm = pl.BlockSpec(memory_space=pltpu.VMEM)
    sm = pl.BlockSpec(memory_space=pltpu.SMEM)
    sems = [pltpu.SemaphoreType.DMA((n,)) for n in (NCOL - 1, NCOL - 1, NROW - 1, NROW - 1, NROW - 1, NROW - 1, NCOL - 1, NCOL - 1, 6, 6)]
    hbm = pl.BlockSpec(memory_space=pl.ANY)
    tile = jax.ShapeDtypeStruct((8, H), F32)
    return pl.pallas_call(
        tail_kernel,
        name="tail",
        out_shape=[jax.ShapeDtypeStruct((2, M, M), F32), tile, tile, jax.ShapeDtypeStruct((2, M, 768), F32)],
        in_specs=[sm, vm, vm, hbm],
        out_specs=[vm, vm, vm, hbm],
        scratch_shapes=[
            pltpu.VMEM((NCOL, H + 16, H), F32),
            pltpu.VMEM((NCOL - 1, H + 16, H), F32),
            pltpu.VMEM((NROW, 24, H), F32),
            pltpu.VMEM((NROW - 1, 24, H), F32),
            pltpu.VMEM((NROW, 8, H), F32),
            pltpu.VMEM((NCOL, NROW, 8, H), F32),
        ]
        + sems,
        compiler_params=pltpu.CompilerParams(collective_id=0, has_side_effects=True),
        cost_estimate=pl.CostEstimate(flops=10**6, bytes_accessed=1 << 20, transcendentals=0),
    )(visits, pacc, stats, halo)


def finish_kernel(upper, coeff, inner, own12, own4, own3, right, down12, down3, out):
    k = pl.program_id(0)
    factor = coeff[0:1, 0:1]

    @pl.when(k < 3)
    def _():
        out[:, :M] = (inner[:, :M] + jnp.where(upper[0] > 0, down12[...], 0.0)) * factor
        out[:, M:] = own12[...] * factor

    @pl.when(k < 2)
    def _():
        out[:, M:] += inner[:, M:] * factor

    @pl.when(k == 3)
    def _():
        out[:, :M] = (own4[...] + down3[...]) * factor
        out[:, M:] = own3[...] * factor

    @pl.when(k == 0)
    def _():
        out[...] += right[...] * factor


def finished(upper, coeff, inner, own12, own4, own3, right, down12, down3):
    block = lambda index: pl.BlockSpec((2, M, M), index)
    return pl.pallas_call(
        finish_kernel,
        name="finished",
        grid=(4,),
        out_shape=jax.ShapeDtypeStruct((2, 512, 1024), F32),
        in_specs=[
            pl.BlockSpec(memory_space=pltpu.SMEM),
            pl.BlockSpec(memory_space=pltpu.VMEM),
            pl.BlockSpec((2, 512, M), lambda k: (0, 0, jnp.minimum(k, 2))),
            block(lambda k: (0, 0, jnp.minimum(k, 2))),
            block(lambda k: (0, 0, 0)),
            block(lambda k: (0, 0, 1)),
            pl.BlockSpec((2, 512, M), lambda k: (0, 0, 0)),
            block(lambda k: (0, 0, jnp.minimum(k, 2))),
            block(lambda k: (0, 0, 0)),
        ],
        out_specs=pl.BlockSpec((2, 512, M), lambda k: (0, 0, k)),
        cost_estimate=pl.CostEstimate(flops=10**7, bytes_accessed=10 << 20, transcendentals=0),
    )(upper, coeff, inner, own12, own4, own3, right, down12, down3)


def passed_along(value, axis, steps):
    count = lax.axis_size(axis)
    first, last = (max(0, -steps), min(count, count - steps))
    return lax.ppermute(value, axis, [(source, source + steps) for source in range(first, last)])


def body(sample, probe, patterns, positions, counts):
    tile_rows, tile_cols = sample.shape[1:]
    row_at, col_at = lax.axis_index("row"), lax.axis_index("col")
    own = counts[row_at * NCOL + col_at]
    pos = positions - jnp.stack([row_at * tile_rows, col_at * tile_cols])[None, :]
    count = own.reshape(1)
    visits = jnp.sum(counts).astype(F32).reshape(1)
    tables = tuple(jnp.asarray(t) for t in dft_tables())
    args = (pos, count, patterns, probe, tables)
    chunk = lambda k: sample[:, :M, k * M : (k + 1) * M]
    first = chunk(0)
    sample, first = lax.optimization_barrier((sample, first))
    low = [passed_along(first, "row", -1), None, None, passed_along(chunk(3), "row", -1)]
    right = passed_along(sample[:, :, :M], "col", -1)
    (inner,), sums = windows(
        "windows_inside", *args, (),
        [(sample, 0, 0, 512, 1024, 0, 0)], [], [(0, 512, 1024, 0)],
        8, 512, 0, 0, lambda o, c: (o <= M) & (c < 768),
    )
    sums, next_low, sample = lax.optimization_barrier((sums, low[0], sample))
    low[2] = passed_along(chunk(2), "row", -1)
    low[1] = passed_along(chunk(1), "row", -1)
    corner = passed_along(next_low, "col", -1)
    (own4, edge, edge_low, part3), sums = windows(
        "windows_right", *args, sums,
        [(sample, 0, 768, 512, M, 0, 0), (right, 0, 0, 512, M, 0, 2), (low[3], 0, 0, M, M, 512, 0), (corner, 0, 0, M, M, 512, 2)],
        [(inner, 0, 768, 512, M, 0, 0)], [(0, 512, M, 0), (0, 512, M, 2), (512, M, M, 2), (512, M, M, 0)],
        4, 768, 0, 768, lambda o, c: c >= 768,
    )
    low_right = passed_along(edge_low, "col", 1)
    came_right = passed_along(edge, "col", 1)
    (own3, halo3, part2), sums = windows(
        "windows_third", *args, sums,
        [(sample, M, 512, M, 512, 0, 0), (low[2], 0, 0, M, M, M, 0), (low[3], 0, 0, M, M, M, 2)],
        [(part3, 0, 0, M, M, M, 2), (own4, M, 0, M, M, 0, 2), (inner, M, 512, M, M, 0, 0)],
        [(0, M, 512, 0), (M, M, M, 2), (M, M, M, 0)],
        4, 512, M, 512, lambda o, c: (o > M) & (c >= 512) & (c < 768),
    )
    down3 = passed_along(halo3, "row", 1)
    (own12, halo12), sums = windows(
        "windows_left", *args, sums,
        [(sample, M, 0, M, 768, 0, 0), (low[0], 0, 0, M, M, M, 0), (low[1], 0, 0, M, M, M, 2), (low[2], 0, 0, M, M, M, 4)],
        [(part2, 0, 0, M, M, M, 4), (low_right, 0, 0, M, M, M, 0), (own3, 0, 0, M, M, 0, 4)],
        [(0, M, 768, 0), (M, M, 768, 0)],
        6, 512, M, 0, lambda o, c: (o > M) & (c < 512),
    )
    probe_grad, coeff, misfit, down12 = tail(visits, *sums, halo12)
    upper = (row_at > 0).astype(jnp.int32).reshape(1)
    object_grad = finished(upper, coeff, inner, own12, own4, own3, came_right, down12, down3)
    return object_grad, probe_grad, misfit[0, 0]


def solution(mesh):
    in_specs = (
        P(None, "row", "col"),
        P(),
        P(("row", "col"), None, None),
        P(("row", "col"), None),
        P(),
    )
    out_specs = (P(None, "row", "col"), P(), P())
    return jax.shard_map(body, mesh=mesh, in_specs=in_specs, out_specs=out_specs, check_vma=False)
```

```python
import math

import jax
import jax.numpy as jnp
import numpy as np
from jax import lax
from jax.experimental import pallas as pl
from jax.experimental.pallas import tpu as pltpu
from jax.sharding import PartitionSpec as P

F32 = jnp.float32
BF16 = jnp.bfloat16
M = 256
H = 128
CAP = 16
SIDE = 2
LAG = 0


def split_table(table):
    high = table.astype(np.float32).astype(jnp.bfloat16)
    low = (table - high.astype(np.float64)).astype(np.float32).astype(jnp.bfloat16)
    return high, low


def dft_tables():
    n = np.arange(H)[:, None]
    m = np.arange(H)[None, :]
    right, left = [], []
    for sign in (-1.0, 1.0):
        for odd in (0, 1):
            if sign < 0:
                angle = 2 * math.pi * (n * (2 * m + odd) % M) / M
            else:
                angle = 2 * math.pi * ((2 * n + odd) * m % M) / M
            re, im = np.cos(angle) / 16.0, sign * np.sin(angle) / 16.0
            high, low = split_table(np.block([[re, im], [-im, re]]))
            right.append(np.concatenate([high, high, low], axis=0))
            re, im = re.T, im.T
            high, low = split_table(np.block([[re, -im], [im, re]]))
            left.append(np.concatenate([high, low, high], axis=1))
    order = np.zeros((M, M), np.float32)
    k = np.arange(M)
    order[k, k // 2 + H * (k % 2)] = 1.0
    order = np.concatenate([order, order], axis=0).astype(jnp.bfloat16)
    return np.stack(right), np.stack(left), order


def split(value):
    high = value.astype(BF16)
    return high, (value - high.astype(F32)).astype(BF16)


def dot(a, b):
    return jnp.dot(a, b, preferred_element_type=F32)


def right_dot(value, table):
    high, low = split(value)
    return dot(jnp.concatenate([high, low, high], axis=1), table)


def left_dot(table, value):
    high, low = split(value)
    return dot(table, jnp.concatenate([high, high, low], axis=0))


def lanes(a, b):
    return jnp.concatenate([a, b], axis=1)


def rows(*parts):
    return jnp.concatenate(parts, axis=0)


def one_window(spot, ext, acc, probe, right, left, order, pacc, stats, rolled, patch):
    top, j0, dc, pat = spot
    lane = lax.broadcasted_iota(jnp.int32, (M, H), 1)
    mask = lane >= dc
    at = pl.ds(top, M)

    def turned(a, b, shift, keep):
        a, b = pltpu.roll(a, shift, 1), pltpu.roll(b, shift, 1)
        return jnp.where(keep, a, b), jnp.where(keep, b, a)

    for p in range(2):
        a, b = turned(probe[p, :, :H], probe[p, :, H:], dc, mask)
        rolled[p, :, :H] = a
        rolled[p, :, H:] = b
        patch[p, :, :H] = jnp.where(mask, ext[p, j0, at, :], ext[p, j0 + 2, at, :])
        patch[p, :, H:] = ext[p, j0 + 1, at, :]
    wave_re = rolled[0] * patch[0] - rolled[1] * patch[1]
    wave_im = rolled[0] * patch[1] + rolled[1] * patch[0]
    sums = lanes(wave_re[:, :H] + wave_re[:, H:], wave_im[:, :H] + wave_im[:, H:])
    difs = lanes(wave_re[:, :H] - wave_re[:, H:], wave_im[:, :H] - wave_im[:, H:])
    yield
    even = right_dot(sums, right[0])
    odd = right_dot(difs, right[1])
    yield
    halves = ((even[:H] + even[H:], odd[:H] + odd[H:]), (even[:H] - even[H:], odd[:H] - odd[H:]))
    fars, levels = [], []
    for parity, (e, o) in enumerate(halves):
        fars.append(left_dot(left[parity], rows(lanes(e[:, :H], o[:, :H]), lanes(e[:, H:], o[:, H:]))))
        every = pl.ds(parity, H, 2)
        level = lanes(pat[0, every, :], pat[1, every, :])
        stats[8:] += jnp.sum(level.reshape(16, 8, M), axis=0)
        high, low = split(level)
        levels.append(dot(lanes(high, low), order[...]))
        yield
    back = []
    for parity, far in enumerate(fars):
        far_re, far_im = far[:H], far[H:]
        resid = far_re * far_re + far_im * far_im - levels[parity]
        stats[:8] += jnp.sum((resid * resid).reshape(16, 8, M), axis=0)
        back.append(left_dot(left[2 + parity], rows(resid * far_re, resid * far_im)))
        yield
    half_s, half_d = back[0] + back[1], back[0] - back[1]
    re, im = rows(half_s[:H], half_d[:H]), rows(half_s[H:], half_d[H:])
    even = right_dot(lanes(re[:, :H], im[:, :H]), right[2])
    odd = right_dot(lanes(re[:, H:], im[:, H:]), right[3])
    yield
    first, second = even + odd, even - odd
    back_re = lanes(first[:, :H], second[:, :H])
    back_im = lanes(first[:, H:], second[:, H:])
    unmask = lane < H - dc
    undo = lax.rem(H - dc, H)
    for p in range(2):
        if p == 0:
            update = rolled[0] * back_re + rolled[1] * back_im
            grad = patch[0] * back_re + patch[1] * back_im
        else:
            update = rolled[0] * back_im - rolled[1] * back_re
            grad = patch[0] * back_im - patch[1] * back_re
        acc[p, j0, at, :] += jnp.where(mask, update[:, :H], 0.0)
        acc[p, j0 + 2, at, :] += jnp.where(mask, 0.0, update[:, :H])
        acc[p, j0 + 1, at, :] += update[:, H:]
        a, b = turned(grad[:, :H], grad[:, H:], undo, unmask)
        pacc[p, :, :H] += a
        pacc[p, :, H:] += b
    yield


def some_windows(spots, ext, acc, probe, right, left, order, pacc, stats, rolled, patch):
    runs = [
        one_window(spot, ext, acc, probe, right, left, order, pacc, stats, rolled.at[w], patch.at[w])
        for w, spot in enumerate(spots)
    ]
    steps = 8
    for t in range(steps + LAG * (len(runs) - 1)):
        for w, run in enumerate(runs):
            if 0 <= t - LAG * w < steps:
                next(run)


def windows_kernel(plan, *refs):
    names = plan["names"]
    at = dict(zip(names, refs))
    ext, acc = at["ext"], at["acc"]
    pos, count = at["pos"], at["count"]
    n_pieces, n_carry = len(plan["pieces"]), len(plan["carry"])
    nblk = plan["nblk"]

    def here(s):
        o, c = pos[s, 0], pos[s, 1]
        return (s < count[0]) & plan["cond"](o, c)

    copies = []

    def begin(src, dst):
        copy = pltpu.make_async_copy(src, dst, at["sems"].at[len(copies)])
        copy.start()
        copies.append(copy)

    def pattern_copies(s):
        return [
            pltpu.make_async_copy(at["patterns"].at[s, :, pl.ds(k * H, H)], at["pat"].at[s, k], at["pat_sems"].at[s, k])
            for k in range(2)
        ]

    for ref, (r0, c0, nr, nc, dr, db) in zip(at["pieces"], plan["pieces"]):
        for k in range(nc // H):
            begin(ref.at[:, pl.ds(r0, nr), pl.ds(c0 + k * H, H)], ext.at[:, db + k, pl.ds(dr, nr), :])
    for ref, (r0, c0, nr, nc, dr, db) in zip(at["carry"], plan["carry"]):
        for k in range(nc // H):
            begin(ref.at[:, pl.ds(r0, nr), pl.ds(c0 + k * H, H)], acc.at[:, db + k, pl.ds(dr, nr), :])

    todo = at["todo"]

    def choose(s, n):
        todo[n] = s

        @pl.when(here(s))
        def _():
            for copy in pattern_copies(s):
                copy.start()

        return n + here(s).astype(jnp.int32)

    chosen = lax.fori_loop(0, CAP, choose, jnp.int32(0))
    for b, first, end in plan["zeros"]:
        acc[:, b, first:end] = jnp.zeros_like(acc[:, b, first:end])
    for name in ("pacc", "stats"):
        at[name][...] = at[name + "_in"][...] if plan["sums"] else jnp.zeros_like(at[name])
    for copy in copies:
        copy.wait()

    def spot(i):
        s = todo[i]
        for copy in pattern_copies(s):
            copy.wait()
        o, c = pos[s, 0] - plan["row0"], pos[s, 1] - plan["col0"]
        return o, c // H, c % H, at["pat"].at[s]

    def run(spots):
        some_windows(spots, ext, acc, at["probe"], at["right"], at["left"],
                     at["order"], at["pacc"], at["stats"], at["rolled"], at["patch"])

    @pl.loop(0, chosen // SIDE)
    def _(i):
        run([spot(SIDE * i + w) for w in range(SIDE)])

    @pl.loop(chosen // SIDE * SIDE, chosen)
    def _(i):
        run([spot(i)])

    ends = []
    for ref, (r0, nr, nc, db) in zip(at["outs"], plan["outs"]):
        for k in range(nc // H):
            copy = pltpu.make_async_copy(acc.at[:, db + k, pl.ds(r0, nr), :], ref.at[:, :, pl.ds(k * H, H)],
                                         at["sems"].at[len(copies) + len(ends)])
            copy.start()
            ends.append(copy)
    for copy in ends:
        copy.wait()


def windows(name, pos, count, patterns, probe, tables, sums, pieces, carry, outs, nblk, nrows, row0, col0, cond, cost=8):
    right, left, order = tables
    vm = pl.BlockSpec(memory_space=pltpu.VMEM)
    sm = pl.BlockSpec(memory_space=pltpu.SMEM)
    hbm = pl.BlockSpec(memory_space=pl.ANY)
    zeros = []
    for b in range(nblk):
        full = sorted((c[5], c[5] + c[3]) for c in carry if c[6] <= b < c[6] + c[4] // H)
        ends = [0] + [x for span in full for x in span] + [nrows]
        zeros += [(b, first, end) for first, end in zip(ends[::2], ends[1::2]) if end > first]
    plan = dict(
        pieces=[p[1:] for p in pieces], carry=[c[1:] for c in carry], outs=outs, nblk=nblk, row0=row0, col0=col0, cond=cond, sums=sums,
        zeros=zeros,
    )
    n_p, n_c, n_o = len(pieces), len(carry), len(outs)
    n_sems = sum(p[4] // H for p in pieces) + sum(c[4] // H for c in carry) + sum(o[2] // H for o in outs)

    def kernel(*refs):
        it = iter(refs)
        take = lambda n: [next(it) for _ in range(n)]
        at = {}
        at["pos"], at["count"], at["patterns"], at["probe"], at["right"], at["left"], at["order"] = take(7)
        at["pacc_in"], at["stats_in"] = take(2) if sums else (None, None)
        at["pieces"], at["carry"], at["outs"] = take(n_p), take(n_c), take(n_o)
        at["pacc"], at["stats"] = take(2)
        at["ext"], at["acc"], at["pat"], at["rolled"], at["patch"], at["sems"], at["pat_sems"], at["todo"] = take(8)
        windows_kernel(dict(plan, names=list(at)), *at.values())

    out = pl.pallas_call(
        kernel,
        name=name,
        out_shape=[jax.ShapeDtypeStruct((2, nr, nc), F32) for _, nr, nc, _ in outs]
        + [jax.ShapeDtypeStruct((2, M, M), F32), jax.ShapeDtypeStruct((16, M), F32)],
        in_specs=[sm, sm, hbm, vm, vm, vm, vm] + [vm] * len(sums) + [hbm] * (n_p + n_c),
        out_specs=[hbm] * n_o + [vm, vm],
        scratch_shapes=[
            pltpu.VMEM((2, nblk, nrows, H), F32),
            pltpu.VMEM((2, nblk, nrows, H), F32),
            pltpu.VMEM((CAP, 2, M, H), F32),
            pltpu.VMEM((SIDE, 2, M, M), F32),
            pltpu.VMEM((SIDE, 2, M, M), F32),
            pltpu.SemaphoreType.DMA((n_sems,)),
            pltpu.SemaphoreType.DMA((CAP, 2)),
            pltpu.SMEM((CAP,), jnp.int32),
        ],
        compiler_params=pltpu.CompilerParams(vmem_limit_bytes=48 << 20),
        cost_estimate=pl.CostEstimate(flops=cost, bytes_accessed=1 << 10, transcendentals=0),
    )(pos, count, patterns, probe, right, left, order, *sums, *[p[0] for p in pieces], *[c[0] for c in carry])
    return out[:n_o], tuple(out[n_o:])


MESH = pl.DeviceIdType.MESH
NROW, NCOL = 16, 8


def send(src, dst, ss, rs, peer):
    copy = pltpu.make_async_remote_copy(src, dst, ss, rs, device_id=peer, device_id_type=MESH)
    copy.start()
    return copy


def columns(k, n=1):
    return pl.ds(k * H, n * H)


def tail_kernel(visits, pacc, stats, halo, inner, edge, edge_low, out, coeff, misfit, down, came, mine1, got1, mine2, got2, part, wide,
                turn, low, s1, r1, s2, r2, s3, r3, s4, r4, ss, rs, ls):
    row, col = lax.axis_index("row"), lax.axis_index("col")

    def col_peer(k):
        return row, lax.rem(col + k, NCOL)

    def row_peer(k):
        return lax.rem(row + k, NROW), col

    barrier = pltpu.get_barrier_semaphore()
    for k in range(1, NCOL):
        pl.semaphore_signal(barrier, inc=1, device_id=col_peer(k), device_id_type=MESH)
    for k in range(1, NROW):
        pl.semaphore_signal(barrier, inc=1, device_id=row_peer(k), device_id_type=MESH)
    own = pltpu.make_async_copy(halo.at[:, :, columns(0, 2)], turn, ls)
    own.start()
    for p in range(2):
        for b in range(2):
            for h in range(2):
                piece = 4 * p + 2 * b + h
                mine1[piece, :H] = pacc[p, h * H : (h + 1) * H, b * H : (b + 1) * H]
                mine1[piece, H:] = stats[:, :H] + stats[:, H:]
    pl.semaphore_wait(barrier, NCOL + NROW - 2)
    number = iter(range(32))

    def go(src, dst, peer):
        n = next(number)
        return send(src, dst, ss.at[n], rs.at[n], peer)

    def lower(k, n=1):
        return go(halo.at[:, :, columns(k, n)], down.at[:, :, columns(k, n)], row_peer(1))

    corner = go(edge_low, low, col_peer(1))
    rest = [lower(5), lower(4)]
    copies = [
        send(mine1.at[lax.rem(col + k, NCOL)], got1.at[k - 1], s1.at[k - 1], r1.at[k - 1], col_peer(k))
        for k in range(1, NCOL)
    ]
    for copy in copies:
        copy.wait()
    total = mine1[col]
    for k in range(NCOL - 1):
        total = total + got1[k]
    for k in range(NROW):
        mine2[k, :8] = total[8 * k : 8 * k + 8]
        mine2[k, 8:] = total[H:]
    copies = [
        send(mine2.at[lax.rem(row + k, NROW)], got2.at[k - 1], s2.at[k - 1], r2.at[k - 1], row_peer(k))
        for k in range(1, NROW)
    ]
    rest += [
        go(inner.at[:, pl.ds(0, M), columns(8, 2)], came.at[:, pl.ds(0, M)], col_peer(1)),
        go(edge, came.at[:, pl.ds(M, M)], col_peer(1)),
        lower(3),
    ]
    own.wait()
    corner.wait_recv()
    turn[...] += jnp.where(col > 0, low[...], 0.0)
    for copy in copies:
        copy.wait()
    total = mine2[row]
    for k in range(NROW - 1):
        total = total + got2[k]
    pixels = M * M * visits[0]
    mean = jnp.full((8, H), jnp.sum(total[16:])) / pixels
    factor = 4.0 / (mean * mean)
    coeff[...] = factor
    misfit[...] = jnp.full((8, H), jnp.sum(total[8:16])) / (mean * mean * pixels)
    part[row] = total[:8] * (factor / visits[0])
    copies = [send(part.at[row], part.at[row], s3.at[k - 1], r3.at[k - 1], row_peer(k)) for k in range(1, NROW)]
    rest.append(lower(2))
    for copy in copies:
        copy.wait()
    copies = [send(part, wide.at[col], s4.at[k - 1], r4.at[k - 1], col_peer(k)) for k in range(1, NCOL)]
    rest.append(go(turn, down.at[:, :, columns(0, 2)], row_peer(1)))
    wide[col] = part[...]
    for copy in copies:
        copy.wait()
    for p in range(2):
        for b in range(2):
            for h in range(2):
                out[p, h * H : (h + 1) * H, b * H : (b + 1) * H] = wide[4 * p + 2 * b + h].reshape(H, H)
    corner.wait_send()
    for copy in rest:
        copy.wait()


def tail(visits, pacc, stats, halo, inner, edge, edge_low):
    vm = pl.BlockSpec(memory_space=pltpu.VMEM)
    sm = pl.BlockSpec(memory_space=pltpu.SMEM)
    hbm = pl.BlockSpec(memory_space=pl.ANY)
    numbers = (NCOL - 1, NCOL - 1, NROW - 1, NROW - 1, NROW - 1, NROW - 1, NCOL - 1, NCOL - 1, 8, 8)
    tile = jax.ShapeDtypeStruct((8, H), F32)
    return pl.pallas_call(
        tail_kernel,
        name="tail",
        out_shape=[
            jax.ShapeDtypeStruct((2, M, M), F32), tile, tile,
            jax.ShapeDtypeStruct((2, M, 768), F32), jax.ShapeDtypeStruct((2, 512, M), F32),
        ],
        in_specs=[sm, vm, vm, hbm, hbm, hbm, hbm],
        out_specs=[vm, vm, vm, hbm, hbm],
        scratch_shapes=[
            pltpu.VMEM((NCOL, H + 16, H), F32),
            pltpu.VMEM((NCOL - 1, H + 16, H), F32),
            pltpu.VMEM((NROW, 24, H), F32),
            pltpu.VMEM((NROW - 1, 24, H), F32),
            pltpu.VMEM((NROW, 8, H), F32),
            pltpu.VMEM((NCOL, NROW, 8, H), F32),
            pltpu.VMEM((2, M, M), F32),
            pltpu.VMEM((2, M, M), F32),
        ]
        + [pltpu.SemaphoreType.DMA((n,)) for n in numbers]
        + [pltpu.SemaphoreType.DMA],
        compiler_params=pltpu.CompilerParams(collective_id=0, has_side_effects=True, vmem_limit_bytes=32 << 20),
        cost_estimate=pl.CostEstimate(flops=40 * 10**9, bytes_accessed=1 << 20, transcendentals=0),
    )(visits, pacc, stats, halo, inner, edge, edge_low)


def finish_kernel(inside, coeff, misfit, probe, inner, own12, own3, came, down12, down3, out, probe_out, misfit_out,
                  tile, down, right, ins, outs):
    top, bottom = pl.ds(0, M), pl.ds(M, M)
    copies = []
    for k in range(4):
        cols, at = columns(2 * k, 2), columns(2 * (k % 3), 2)
        pairs = [
            (inner.at[:, top, cols], tile.at[:, top, cols]),
            ((own12 if k < 3 else own3).at[:, :, at], tile.at[:, bottom, cols]),
            ((down12 if k < 3 else down3).at[:, :, at], down.at[:, :, cols]),
        ]
        if k == 0:
            pairs.append((came, right))
        copies.append([pltpu.make_async_copy(src, dst, ins.at[k, n]) for n, (src, dst) in enumerate(pairs)])
    for copy in copies[1] + copies[2] + copies[3] + copies[0]:
        copy.start()
    probe_out[...] = probe[...]
    misfit_out[...] = misfit[0:1, 0:1]
    factor = coeff[0:1, 0:1]
    ends = []
    for k in (1, 2, 3, 0):
        cols = columns(2 * k, 2)
        for copy in copies[k]:
            copy.wait()
        came_down = down[:, :, cols] if k == 3 else jnp.where(inside[0] > 0, down[:, :, cols], 0.0)
        upper, lower = tile[:, top, cols] + came_down, tile[:, bottom, cols]
        if k == 0:
            upper = upper + jnp.where(inside[1] > 0, right[:, top], 0.0)
            lower = lower + jnp.where(inside[1] > 0, right[:, bottom], 0.0)
        tile[:, top, cols] = upper * factor
        tile[:, bottom, cols] = lower * factor
        ends.append(pltpu.make_async_copy(tile.at[:, :, cols], out.at[:, :, cols], outs.at[k]))
        ends[-1].start()
    for copy in ends:
        copy.wait()


def finished(inside, coeff, misfit, probe, inner, own12, own3, came, down12, down3):
    vm = pl.BlockSpec(memory_space=pltpu.VMEM)
    sm = pl.BlockSpec(memory_space=pltpu.SMEM)
    hbm = pl.BlockSpec(memory_space=pl.ANY)
    return pl.pallas_call(
        finish_kernel,
        name="finished",
        out_shape=[
            jax.ShapeDtypeStruct((2, 512, 1024), F32),
            jax.ShapeDtypeStruct((2, M, M), F32),
            jax.ShapeDtypeStruct((1, 1), F32),
        ],
        in_specs=[sm, vm, vm, vm] + [hbm] * 6,
        out_specs=[hbm, vm, vm],
        scratch_shapes=[
            pltpu.VMEM((2, 512, 1024), F32),
            pltpu.VMEM((2, M, 1024), F32),
            pltpu.VMEM((2, 512, M), F32),
            pltpu.SemaphoreType.DMA((4, 4)),
            pltpu.SemaphoreType.DMA((4,)),
        ],
        compiler_params=pltpu.CompilerParams(vmem_limit_bytes=32 << 20),
        cost_estimate=pl.CostEstimate(flops=10**7, bytes_accessed=10 << 20, transcendentals=0),
    )(inside, coeff, misfit, probe, inner, own12, own3, came, down12, down3)


def passed_along(value, axis, steps):
    count = lax.axis_size(axis)
    first, last = (max(0, -steps), min(count, count - steps))
    return lax.ppermute(value, axis, [(source, source + steps) for source in range(first, last)])


def body(sample, probe, patterns, positions, counts):
    row_at, col_at = lax.axis_index("row"), lax.axis_index("col")
    first = sample[:, :M, :M]
    later, first = lax.optimization_barrier((sample, first))
    low0 = passed_along(first, "row", -1)
    low32 = passed_along(later[:, :M, 512:], "row", -1)
    low1 = passed_along(later[:, :M, M:512], "row", -1)
    right = passed_along(later[:, :, :M], "col", -1)
    pos = positions - jnp.stack([row_at * 512, col_at * 1024])[None, :]
    count = counts[row_at * NCOL + col_at].reshape(1)
    visits = jnp.sum(counts).astype(F32).reshape(1)
    inside = jnp.stack([row_at > 0, col_at > 0]).astype(jnp.int32)
    args = (pos, count, patterns, probe, tuple(jnp.asarray(t) for t in dft_tables()))
    (inner,), sums = windows(
        "windows_upper", *args, (),
        [(sample, 0, 0, 512, 1024, 0, 0), (right, 0, 0, 512, M, 0, 8)], [], [(0, 512, 1280, 0)],
        10, 512, 0, 0, lambda o, c: o <= M,
    )
    sums, low0 = lax.optimization_barrier((sums, low0))
    corner = passed_along(low0, "col", -1)
    (own3, halo3, part2, bottom2, edge, edge_low), sums = windows(
        "windows_right", *args, sums,
        [(sample, M, 512, M, 512, 0, 0), (right, M, 0, M, M, 0, 4), (low32, 0, 0, M, 512, M, 0), (corner, 0, 0, M, M, M, 4)],
        [(inner, M, 512, M, 768, 0, 0)],
        [(0, M, M, 2), (M, M, M, 2), (M, M, M, 0), (0, M, M, 0), (0, M, M, 4), (M, M, M, 4)],
        6, 512, M, 512, lambda o, c: (o > M) & (c >= 512),
    )
    down3 = passed_along(halo3, "row", 1)
    (own12, halo12), sums = windows(
        "windows_left", *args, sums,
        [(sample, M, 0, M, 768, 0, 0), (low0, 0, 0, M, M, M, 0), (low1, 0, 0, M, M, M, 2), (low32, 0, 0, M, M, M, 4)],
        [(part2, 0, 0, M, M, M, 4), (bottom2, 0, 0, M, M, 0, 4), (inner, M, 0, M, 512, 0, 0)],
        [(0, M, 768, 0), (M, M, 768, 0)],
        6, 512, M, 0, lambda o, c: (o > M) & (c < 512),
    )
    probe_sum, coeff, misfit, down12, came = tail(visits, *sums, halo12, inner, edge, edge_low)
    object_grad, probe_grad, mean_misfit = finished(inside, coeff, misfit, probe_sum, inner, own12, own3, came, down12, down3)
    return object_grad, probe_grad, mean_misfit.reshape(())


def solution(mesh):
    in_specs = (
        P(None, "row", "col"),
        P(),
        P(("row", "col"), None, None),
        P(("row", "col"), None),
        P(),
    )
    out_specs = (P(None, "row", "col"), P(), P())
    return jax.shard_map(body, mesh=mesh, in_specs=in_specs, out_specs=out_specs, check_vma=False)
```

```python
import math

import jax
import jax.numpy as jnp
import numpy as np
from jax import lax
from jax.experimental import pallas as pl
from jax.experimental.pallas import tpu as pltpu
from jax.sharding import PartitionSpec as P

F32 = jnp.float32
BF16 = jnp.bfloat16
M = 256
H = 128
CAP = 16
SIDE = 2
LAG = 0


def dft_tables():
    n = np.arange(H)[:, None]
    m = np.arange(H)[None, :]
    right, left = [], []
    for sign in (-1.0, 1.0):
        for odd in (0, 1):
            if sign < 0:
                angle = 2 * math.pi * (n * (2 * m + odd) % M) / M
            else:
                angle = 2 * math.pi * ((2 * n + odd) * m % M) / M
            re, im = np.cos(angle) / 16.0, sign * np.sin(angle) / 16.0
            right.append(np.block([[re, im], [-im, re]]))
            left.append(right[-1].T)
    order = np.zeros((M, M), np.float32)
    k = np.arange(M)
    order[k, k // 2 + H * (k % 2)] = 1.0
    return np.stack(right).astype(np.float32), np.stack(left).astype(np.float32), order


def split(value):
    high = value.astype(BF16)
    return high, (value - high.astype(F32)).astype(BF16)


def dot(a, b):
    return jnp.dot(a, b, preferred_element_type=F32)


def right_dot(value, table):
    high, low = split(value)
    return dot(high, table[0]) + dot(low, table[0]) + dot(high, table[1])


def left_dot(table, value):
    high, low = split(value)
    return dot(table[0], high) + dot(table[0], low) + dot(table[1], high)


def lanes(a, b):
    return jnp.concatenate([a, b], axis=1)


def rows(*parts):
    return jnp.concatenate(parts, axis=0)


def one_window(spot, ext, acc, probe, right, left, order, pacc, stats, rolled, patch):
    top, j0, dc, pat = spot
    lane = lax.broadcasted_iota(jnp.int32, (M, H), 1)
    mask = lane >= dc
    at = pl.ds(top, M)

    def turned(a, b, shift, keep):
        a, b = pltpu.roll(a, shift, 1), pltpu.roll(b, shift, 1)
        return jnp.where(keep, a, b), jnp.where(keep, b, a)

    for p in range(2):
        a, b = turned(probe[p, :, :H], probe[p, :, H:], dc, mask)
        rolled[p, :, :H] = a
        rolled[p, :, H:] = b
        patch[p, :, :H] = jnp.where(mask, ext[p, j0, at, :], ext[p, j0 + 2, at, :])
        patch[p, :, H:] = ext[p, j0 + 1, at, :]
    wave_re = rolled[0] * patch[0] - rolled[1] * patch[1]
    wave_im = rolled[0] * patch[1] + rolled[1] * patch[0]
    sums = lanes(wave_re[:, :H] + wave_re[:, H:], wave_im[:, :H] + wave_im[:, H:])
    difs = lanes(wave_re[:, :H] - wave_re[:, H:], wave_im[:, :H] - wave_im[:, H:])
    yield
    even = right_dot(sums, right[0])
    odd = right_dot(difs, right[1])
    yield
    halves = ((even[:H] + even[H:], odd[:H] + odd[H:]), (even[:H] - even[H:], odd[:H] - odd[H:]))
    fars, levels = [], []
    for parity, (e, o) in enumerate(halves):
        fars.append(left_dot(left[parity], rows(lanes(e[:, :H], o[:, :H]), lanes(e[:, H:], o[:, H:]))))
        every = pl.ds(parity, H, 2)
        level = lanes(pat[0, every, :], pat[1, every, :])
        stats[8:] += jnp.sum(level.reshape(16, 8, M), axis=0)
        high, low = split(level)
        levels.append(dot(high, order[...]) + dot(low, order[...]))
        yield
    back = []
    for parity, far in enumerate(fars):
        far_re, far_im = far[:H], far[H:]
        resid = far_re * far_re + far_im * far_im - levels[parity]
        stats[:8] += jnp.sum((resid * resid).reshape(16, 8, M), axis=0)
        back.append(left_dot(left[2 + parity], rows(resid * far_re, resid * far_im)))
        yield
    half_s, half_d = back[0] + back[1], back[0] - back[1]
    re, im = rows(half_s[:H], half_d[:H]), rows(half_s[H:], half_d[H:])
    even = right_dot(lanes(re[:, :H], im[:, :H]), right[2])
    odd = right_dot(lanes(re[:, H:], im[:, H:]), right[3])
    yield
    first, second = even + odd, even - odd
    back_re = lanes(first[:, :H], second[:, :H])
    back_im = lanes(first[:, H:], second[:, H:])
    unmask = lane < H - dc
    undo = lax.rem(H - dc, H)
    for p in range(2):
        if p == 0:
            update = rolled[0] * back_re + rolled[1] * back_im
            grad = patch[0] * back_re + patch[1] * back_im
        else:
            update = rolled[0] * back_im - rolled[1] * back_re
            grad = patch[0] * back_im - patch[1] * back_re
        acc[p, j0, at, :] += jnp.where(mask, update[:, :H], 0.0)
        acc[p, j0 + 2, at, :] += jnp.where(mask, 0.0, update[:, :H])
        acc[p, j0 + 1, at, :] += update[:, H:]
        a, b = turned(grad[:, :H], grad[:, H:], undo, unmask)
        pacc[p, :, :H] += a
        pacc[p, :, H:] += b
    yield


def some_windows(spots, ext, acc, probe, right, left, order, pacc, stats, rolled, patch):
    runs = [
        one_window(spot, ext, acc, probe, right, left, order, pacc, stats, rolled.at[w], patch.at[w])
        for w, spot in enumerate(spots)
    ]
    steps = 8
    for t in range(steps + LAG * (len(runs) - 1)):
        for w, run in enumerate(runs):
            if 0 <= t - LAG * w < steps:
                next(run)


def windows_kernel(plan, at):
    ext, acc = at["ext"], at["acc"]
    row, col = lax.axis_index("row"), lax.axis_index("col")
    first_row, first_col = row * 512, col * 1024
    count = at["counts"][row * 8 + col]

    def corner(s):
        return at["pos"][s, 0] - first_row, at["pos"][s, 1] - first_col

    copies = []

    def begin(src, dst):
        copy = pltpu.make_async_copy(src, dst, at["sems"].at[len(copies)])
        copy.start()
        copies.append(copy)

    def pattern_copies(s):
        return [
            pltpu.make_async_copy(at["patterns"].at[s, :, pl.ds(k * H, H)], at["pat"].at[s, k], at["pat_sems"].at[s, k])
            for k in range(2)
        ]

    for ref, (r0, c0, nr, nc, dr, db) in zip(at["pieces"], plan["pieces"]):
        for k in range(nc // H):
            begin(ref.at[:, pl.ds(r0, nr), pl.ds(c0 + k * H, H)], ext.at[:, db + k, pl.ds(dr, nr), :])

    @pl.loop(0, count)
    def _(s):
        for copy in pattern_copies(s):
            copy.start()

    for k in range(4):
        for name in ("right", "left"):
            at[name][k, 0], at[name][k, 1] = split(at[name + "_in"][k])
    at["order"][...] = at["order_in"][...].astype(BF16)
    for name in ("acc", "pacc", "stats"):
        at[name][...] = jnp.zeros_like(at[name])
    for copy in copies:
        copy.wait()

    @pl.when(row == 15)
    def _():
        ext[:, :, 512:] = jnp.zeros_like(ext[:, :, 512:])

    @pl.when(col == 7)
    def _():
        ext[:, 8:] = jnp.zeros_like(ext[:, 8:])

    def spot(i):
        for copy in pattern_copies(i):
            copy.wait()
        o, c = corner(i)
        return o, c // H, c % H, at["pat"].at[i]

    def run(spots):
        some_windows(spots, ext, acc, at["probe"], at["right"], at["left"],
                     at["order"], at["pacc"], at["stats"], at["rolled"], at["patch"])

    @pl.loop(0, count // SIDE)
    def _(i):
        run([spot(SIDE * i + w) for w in range(SIDE)])

    @pl.loop(count // SIDE * SIDE, count)
    def _(i):
        run([spot(i)])

    ends = []
    for ref, (r0, nr, nc, db) in zip(at["outs"], plan["outs"]):
        for k in range(nc // H):
            copy = pltpu.make_async_copy(acc.at[:, db + k, pl.ds(r0, nr), :], ref.at[:, :, pl.ds(k * H, H)],
                                         at["sems"].at[len(copies) + len(ends)])
            copy.start()
            ends.append(copy)
    for copy in ends:
        copy.wait()


def windows(pos, counts, patterns, probe, tables, pieces, outs, nblk, nrows):
    vm = pl.BlockSpec(memory_space=pltpu.VMEM)
    sm = pl.BlockSpec(memory_space=pltpu.SMEM)
    hbm = pl.BlockSpec(memory_space=pl.ANY)
    plan = dict(pieces=[p[1:] for p in pieces], outs=outs)
    n_p, n_o = len(pieces), len(outs)
    n_sems = sum(p[4] // H for p in pieces) + sum(o[2] // H for o in outs)

    def kernel(*refs):
        it = iter(refs)
        take = lambda n: [next(it) for _ in range(n)]
        at = {}
        at["pos"], at["counts"], at["patterns"], at["probe"], at["right_in"], at["left_in"], at["order_in"] = take(7)
        at["pieces"], at["outs"] = take(n_p), take(n_o)
        at["pacc"], at["stats"] = take(2)
        at["ext"], at["acc"], at["pat"], at["rolled"], at["patch"], at["right"], at["left"], at["order"] = take(8)
        at["sems"], at["pat_sems"] = take(2)
        windows_kernel(plan, at)

    out = pl.pallas_call(
        kernel,
        name="windows",
        out_shape=[jax.ShapeDtypeStruct((2, nr, nc), F32) for _, nr, nc, _ in outs]
        + [jax.ShapeDtypeStruct((2, M, M), F32), jax.ShapeDtypeStruct((16, M), F32)],
        in_specs=[sm, sm, hbm, vm, vm, vm, vm] + [hbm] * n_p,
        out_specs=[hbm] * n_o + [vm, vm],
        scratch_shapes=[
            pltpu.VMEM((2, nblk, nrows, H), F32),
            pltpu.VMEM((2, nblk, nrows, H), F32),
            pltpu.VMEM((CAP, 2, M, H), F32),
            pltpu.VMEM((SIDE, 2, M, M), F32),
            pltpu.VMEM((SIDE, 2, M, M), F32),
            pltpu.VMEM((4, 2, M, M), BF16),
            pltpu.VMEM((4, 2, M, M), BF16),
            pltpu.VMEM((M, M), BF16),
            pltpu.SemaphoreType.DMA((n_sems,)),
            pltpu.SemaphoreType.DMA((CAP, 2)),
        ],
        compiler_params=pltpu.CompilerParams(vmem_limit_bytes=34 << 20),
        cost_estimate=pl.CostEstimate(flops=12 * 10**9, bytes_accessed=8 << 20, transcendentals=0),
    )(pos, counts, patterns, probe, *tables, *[p[0] for p in pieces])
    return out[:n_o], tuple(out[n_o:])


MESH = pl.DeviceIdType.MESH
NROW, NCOL = 16, 8


def send(src, dst, ss, rs, peer):
    copy = pltpu.make_async_remote_copy(src, dst, ss, rs, device_id=peer, device_id_type=MESH)
    copy.start()
    return copy


def ring(row, step):
    return row // 4 * 4 + lax.rem(row + step + 4, 4)


def columns(k, n=1):
    return pl.ds(k * H, n * H)


def halo_kernel(sample, low, right, corner, held1, held2, ss, rs):
    row, col = lax.axis_index("row"), lax.axis_index("col")
    above, below = lax.rem(row + NROW - 1, NROW), lax.rem(row + 1, NROW)
    before, after = lax.rem(col + NCOL - 1, NCOL), lax.rem(col + 1, NCOL)
    across, back = ring(above, 2), lax.rem(ring(row, 2) + 1, NROW)
    barrier = pltpu.get_barrier_semaphore()
    for peer in ((below, col), (ring(row, -1), col), (back, col), (row, after)):
        pl.semaphore_signal(barrier, inc=1, device_id=peer, device_id_type=MESH)
    pl.semaphore_wait(barrier, 4)
    number = iter(range(32))

    def go(src, dst, peer):
        n = next(number)
        return send(src, dst, ss.at[n], rs.at[n], peer)

    top = pl.ds(0, M)
    up = ring(row, 1), col
    hop1 = [go(sample.at[:, top, columns(2 + i)], held1.at[i], (across, col)) for i in range(2)]
    first = go(sample.at[:, top, columns(0, 2)], low.at[:, :, columns(0, 2)], (above, col))
    rest = [go(sample.at[:, :, columns(0, 2)], right, (row, before))]
    rest += [go(sample.at[:, top, columns(k, 2)], low.at[:, :, columns(k, 2)], (above, col)) for k in (4, 6)]
    hop1[0].wait_recv()
    hop2 = [go(held1.at[0], held2.at[0], up)]
    first.wait_recv()
    rest.append(go(low.at[:, :, columns(0, 2)], corner, (row, before)))
    hop1[1].wait_recv()
    hop2.append(go(held1.at[1], held2.at[1], up))
    hop3 = []
    for i in range(2):
        hop2[i].wait_recv()
        hop3.append(go(held2.at[i], low.at[:, :, columns(2 + i)], up))
    for copy in [first] + hop1 + hop2:
        copy.wait_send()
    for copy in rest + hop3:
        copy.wait()


def halos(sample):
    hbm = pl.BlockSpec(memory_space=pl.ANY)
    return pl.pallas_call(
        halo_kernel,
        name="halos",
        out_shape=[
            jax.ShapeDtypeStruct((2, M, 1024), F32),
            jax.ShapeDtypeStruct((2, 512, M), F32),
            jax.ShapeDtypeStruct((2, M, M), F32),
        ],
        in_specs=[pl.BlockSpec(memory_space=pltpu.HBM)],
        out_specs=[hbm] * 3,
        scratch_shapes=[
            pltpu.VMEM((2, 2, M, H), F32),
            pltpu.VMEM((2, 2, M, H), F32),
            pltpu.SemaphoreType.DMA((11,)),
            pltpu.SemaphoreType.DMA((11,)),
        ],
        compiler_params=pltpu.CompilerParams(collective_id=1, has_side_effects=True, vmem_limit_bytes=14 << 20),
        cost_estimate=pl.CostEstimate(flops=40 * 10**9, bytes_accessed=1 << 20, transcendentals=0),
    )(sample)


def tail_kernel(counts, pacc, stats, halo, edge, edge_low, out, coeff, misfit, down, came, mine1, got1, mine2, got2, part, wide,
                turn, low, held1, held2, s1, r1, s2, r2, s3, r3, s4, r4, ss, rs, ls):
    row, col = lax.axis_index("row"), lax.axis_index("col")

    def col_peer(k):
        return row, lax.rem(col + k, NCOL)

    def row_peer(k):
        return lax.rem(row + k, NROW), col

    barrier = pltpu.get_barrier_semaphore()
    for k in range(1, NCOL):
        pl.semaphore_signal(barrier, inc=1, device_id=col_peer(k), device_id_type=MESH)
    for k in range(1, NROW):
        pl.semaphore_signal(barrier, inc=1, device_id=row_peer(k), device_id_type=MESH)
    own = pltpu.make_async_copy(halo.at[:, :, columns(0, 2)], turn, ls)
    own.start()
    for p in range(2):
        for b in range(2):
            for h in range(2):
                piece = 4 * p + 2 * b + h
                mine1[piece, :H] = pacc[p, h * H : (h + 1) * H, b * H : (b + 1) * H]
                mine1[piece, H:] = stats[:, :H] + stats[:, H:]
    pl.semaphore_wait(barrier, NCOL + NROW - 2)
    number = iter(range(32))

    def go(src, dst, peer):
        n = next(number)
        return send(src, dst, ss.at[n], rs.at[n], peer)

    def lower(k, n=1):
        return go(halo.at[:, :, columns(k, n)], down.at[:, :, columns(k, n)], row_peer(1))

    across, back = (ring(lax.rem(row + 1, NROW), 2), col), (ring(row, -1), col)
    hop1 = [go(halo.at[:, :, columns(2 + i)], held1.at[i], across) for i in range(2)]
    rest = [lower(7), lower(6)]
    copies = [
        send(mine1.at[lax.rem(col + k, NCOL)], got1.at[k - 1], s1.at[k - 1], r1.at[k - 1], col_peer(k))
        for k in range(1, NCOL)
    ]
    hop1[0].wait_recv()
    hop2 = [go(held1.at[0], held2.at[0], back)]
    for copy in copies:
        copy.wait()
    total = mine1[col]
    for k in range(NCOL - 1):
        total = total + got1[k]
    for k in range(NROW):
        mine2[k, :8] = total[8 * k : 8 * k + 8]
        mine2[k, 8:] = total[H:]
    copies = [
        send(mine2.at[lax.rem(row + k, NROW)], got2.at[k - 1], s2.at[k - 1], r2.at[k - 1], row_peer(k))
        for k in range(1, NROW)
    ]
    corner = go(edge_low, low, col_peer(1))
    rest.append(lower(5))
    hop1[1].wait_recv()
    hop2.append(go(held1.at[1], held2.at[1], back))
    rest.append(go(edge, came, col_peer(1)))
    for copy in copies:
        copy.wait()
    total = mine2[row]
    for k in range(NROW - 1):
        total = total + got2[k]
    visits = jnp.sum(counts[...].astype(F32))
    pixels = M * M * visits
    mean = jnp.full((8, H), jnp.sum(total[16:])) / pixels
    factor = 4.0 / (mean * mean)
    coeff[...] = factor
    misfit[...] = jnp.full((8, H), jnp.sum(total[8:16])) / (mean * mean * pixels)
    part[row] = total[:8] * (factor / visits)
    copies = [send(part.at[row], part.at[row], s3.at[k - 1], r3.at[k - 1], row_peer(k)) for k in range(1, NROW)]
    rest.append(lower(4))
    hop2[0].wait_recv()
    hop3 = [go(held2.at[0], down.at[:, :, columns(2)], back)]
    own.wait()
    corner.wait_recv()
    turn[...] += jnp.where(col > 0, low[...], 0.0)
    rest.append(go(turn, down.at[:, :, columns(0, 2)], row_peer(1)))
    for copy in copies:
        copy.wait()
    copies = [send(part, wide.at[col], s4.at[k - 1], r4.at[k - 1], col_peer(k)) for k in range(1, NCOL)]
    wide[col] = part[...]
    hop2[1].wait_recv()
    hop3.append(go(held2.at[1], down.at[:, :, columns(3)], back))
    for copy in copies:
        copy.wait()
    for p in range(2):
        for b in range(2):
            for h in range(2):
                out[p, h * H : (h + 1) * H, b * H : (b + 1) * H] = wide[4 * p + 2 * b + h].reshape(H, H)
    for copy in [corner] + hop1 + hop2:
        copy.wait_send()
    for copy in rest + hop3:
        copy.wait()


def tail(counts, pacc, stats, halo, edge, edge_low):
    vm = pl.BlockSpec(memory_space=pltpu.VMEM)
    sm = pl.BlockSpec(memory_space=pltpu.SMEM)
    hbm = pl.BlockSpec(memory_space=pl.ANY)
    numbers = (NCOL - 1, NCOL - 1, NROW - 1, NROW - 1, NROW - 1, NROW - 1, NCOL - 1, NCOL - 1, 13, 13)
    tile = jax.ShapeDtypeStruct((8, H), F32)
    return pl.pallas_call(
        tail_kernel,
        name="tail",
        out_shape=[
            jax.ShapeDtypeStruct((2, M, M), F32), tile, tile,
            jax.ShapeDtypeStruct((2, M, 1024), F32), jax.ShapeDtypeStruct((2, 512, M), F32),
        ],
        in_specs=[vm, vm, vm, hbm, hbm, hbm],
        out_specs=[vm, vm, vm, hbm, hbm],
        scratch_shapes=[
            pltpu.VMEM((NCOL, H + 16, H), F32),
            pltpu.VMEM((NCOL - 1, H + 16, H), F32),
            pltpu.VMEM((NROW, 24, H), F32),
            pltpu.VMEM((NROW - 1, 24, H), F32),
            pltpu.VMEM((NROW, 8, H), F32),
            pltpu.VMEM((NCOL, NROW, 8, H), F32),
            pltpu.VMEM((2, M, M), F32),
            pltpu.VMEM((2, M, M), F32),
            pltpu.VMEM((2, 2, M, H), F32),
            pltpu.VMEM((2, 2, M, H), F32),
        ]
        + [pltpu.SemaphoreType.DMA((n,)) for n in numbers]
        + [pltpu.SemaphoreType.DMA],
        compiler_params=pltpu.CompilerParams(collective_id=0, has_side_effects=True, vmem_limit_bytes=14 << 20),
        cost_estimate=pl.CostEstimate(flops=40 * 10**9, bytes_accessed=1 << 20, transcendentals=0),
    )(counts, pacc, stats, halo, edge, edge_low)


def finish_kernel(coeff, misfit, probe, own, came, came_down, out, probe_out, misfit_out,
                  tile, down, right, ins, outs):
    row, col = lax.axis_index("row"), lax.axis_index("col")
    top, bottom = pl.ds(0, M), pl.ds(M, M)
    copies = []
    for k in range(4):
        cols = columns(2 * k, 2)
        pairs = [(own.at[:, :, cols], tile.at[:, :, cols]), (came_down.at[:, :, cols], down.at[:, :, cols])]
        if k == 0:
            pairs.append((came, right))
        copies.append([pltpu.make_async_copy(src, dst, ins.at[k, n]) for n, (src, dst) in enumerate(pairs)])
    for copy in copies[1] + copies[2] + copies[3] + copies[0]:
        copy.start()
    probe_out[...] = probe[...]
    misfit_out[...] = misfit[0:1, 0:1]
    factor = coeff[0:1, 0:1]
    ends = []
    for k in (1, 2, 3, 0):
        cols = columns(2 * k, 2)
        for copy in copies[k]:
            copy.wait()
        upper = tile[:, top, cols] + jnp.where(row > 0, down[:, :, cols], 0.0)
        lower = tile[:, bottom, cols]
        if k == 0:
            upper = upper + jnp.where(col > 0, right[:, top], 0.0)
            lower = lower + jnp.where(col > 0, right[:, bottom], 0.0)
        tile[:, top, cols] = upper * factor
        tile[:, bottom, cols] = lower * factor
        ends.append(pltpu.make_async_copy(tile.at[:, :, cols], out.at[:, :, cols], outs.at[k]))
        ends[-1].start()
    for copy in ends:
        copy.wait()


def finished(coeff, misfit, probe, own, came, down):
    vm = pl.BlockSpec(memory_space=pltpu.VMEM)
    hbm = pl.BlockSpec(memory_space=pl.ANY)
    return pl.pallas_call(
        finish_kernel,
        name="finished",
        out_shape=[
            jax.ShapeDtypeStruct((2, 512, 1024), F32),
            jax.ShapeDtypeStruct((2, M, M), F32),
            jax.ShapeDtypeStruct((1, 1), F32),
        ],
        in_specs=[vm, vm, vm] + [hbm] * 3,
        out_specs=[hbm, vm, vm],
        scratch_shapes=[
            pltpu.VMEM((2, 512, 1024), F32),
            pltpu.VMEM((2, M, 1024), F32),
            pltpu.VMEM((2, 512, M), F32),
            pltpu.SemaphoreType.DMA((4, 3)),
            pltpu.SemaphoreType.DMA((4,)),
        ],
        compiler_params=pltpu.CompilerParams(vmem_limit_bytes=14 << 20),
        cost_estimate=pl.CostEstimate(flops=10**7, bytes_accessed=10 << 20, transcendentals=0),
    )(coeff, misfit, probe, own, came, down)


def body(sample, probe, patterns, positions, counts):
    tables = tuple(jnp.asarray(t) for t in dft_tables())
    low, right, corner = halos(sample)
    (own, halo, edge, edge_low), sums = windows(
        positions, counts, patterns, probe, tables,
        [(sample, 0, 0, 512, 1024, 0, 0), (right, 0, 0, 512, M, 0, 8), (low, 0, 0, M, 1024, 512, 0), (corner, 0, 0, M, M, 512, 8)],
        [(0, 512, 1024, 0), (512, M, 1024, 0), (0, 512, M, 8), (512, M, M, 8)],
        10, 768,
    )
    probe_sum, coeff, misfit, down, came = tail(counts.reshape(1, H), *sums, halo, edge, edge_low)
    object_grad, probe_grad, mean_misfit = finished(coeff, misfit, probe_sum, own, came, down)
    return object_grad, probe_grad, mean_misfit.reshape(())


def solution(mesh):
    in_specs = (
        P(None, "row", "col"),
        P(),
        P(("row", "col"), None, None),
        P(("row", "col"), None),
        P(),
    )
    out_specs = (P(None, "row", "col"), P(), P())
    return jax.shard_map(body, mesh=mesh, in_specs=in_specs, out_specs=out_specs, check_vma=False)
```

```python
import math

import jax
import jax.numpy as jnp
import numpy as np
from jax import lax
from jax.experimental import pallas as pl
from jax.experimental.pallas import tpu as pltpu
from jax.sharding import PartitionSpec as P

F32 = jnp.float32
BF16 = jnp.bfloat16
M = 256
H = 128
CAP = 16
SIDE = 2
LAG = 0


def dft_tables():
    n = np.arange(H)[:, None]
    m = np.arange(H)[None, :]
    right, left = [], []
    for sign in (-1.0, 1.0):
        for odd in (0, 1):
            if sign < 0:
                angle = 2 * math.pi * (n * (2 * m + odd) % M) / M
            else:
                angle = 2 * math.pi * ((2 * n + odd) * m % M) / M
            re, im = np.cos(angle) / 16.0, sign * np.sin(angle) / 16.0
            right.append(np.block([[re, im], [-im, re]]))
            left.append(right[-1].T)
    order = np.zeros((M, M), np.float32)
    k = np.arange(M)
    order[k, k // 2 + H * (k % 2)] = 1.0
    return np.stack(right).astype(np.float32), np.stack(left).astype(np.float32), order


def split(value):
    high = value.astype(BF16)
    return high, (value - high.astype(F32)).astype(BF16)


def dot(a, b):
    return jnp.dot(a, b, preferred_element_type=F32)


def right_dot(value, table):
    high, low = split(value)
    return dot(high, table[0]) + dot(low, table[0]) + dot(high, table[1])


def left_dot(table, value):
    high, low = split(value)
    return dot(table[0], high) + dot(table[0], low) + dot(table[1], high)


def lanes(a, b):
    return jnp.concatenate([a, b], axis=1)


def rows(*parts):
    return jnp.concatenate(parts, axis=0)


def one_window(spot, ext, acc, probe, right, left, order, pacc, stats, rolled, patch):
    top, j0, dc, pat = spot
    lane = lax.broadcasted_iota(jnp.int32, (M, H), 1)
    mask = lane >= dc
    at = pl.ds(top, M)

    def turned(a, b, shift, keep):
        a, b = pltpu.roll(a, shift, 1), pltpu.roll(b, shift, 1)
        return jnp.where(keep, a, b), jnp.where(keep, b, a)

    for p in range(2):
        a, b = turned(probe[p, :, :H], probe[p, :, H:], dc, mask)
        rolled[p, :, :H] = a
        rolled[p, :, H:] = b
        patch[p, :, :H] = jnp.where(mask, ext[p, j0, at, :], ext[p, j0 + 2, at, :])
        patch[p, :, H:] = ext[p, j0 + 1, at, :]
    wave_re = rolled[0] * patch[0] - rolled[1] * patch[1]
    wave_im = rolled[0] * patch[1] + rolled[1] * patch[0]
    sums = lanes(wave_re[:, :H] + wave_re[:, H:], wave_im[:, :H] + wave_im[:, H:])
    difs = lanes(wave_re[:, :H] - wave_re[:, H:], wave_im[:, :H] - wave_im[:, H:])
    yield
    even = right_dot(sums, right[0])
    odd = right_dot(difs, right[1])
    yield
    halves = ((even[:H] + even[H:], odd[:H] + odd[H:]), (even[:H] - even[H:], odd[:H] - odd[H:]))
    fars, levels = [], []
    for parity, (e, o) in enumerate(halves):
        fars.append(left_dot(left[parity], rows(lanes(e[:, :H], o[:, :H]), lanes(e[:, H:], o[:, H:]))))
        every = pl.ds(parity, H, 2)
        level = lanes(pat[0, every, :], pat[1, every, :])
        stats[8:] += jnp.sum(level.reshape(16, 8, M), axis=0)
        high, low = split(level)
        levels.append(dot(high, order[...]) + dot(low, order[...]))
    yield
    back = []
    for parity, far in enumerate(fars):
        far_re, far_im = far[:H], far[H:]
        resid = far_re * far_re + far_im * far_im - levels[parity]
        stats[:8] += jnp.sum((resid * resid).reshape(16, 8, M), axis=0)
        back.append(left_dot(left[2 + parity], rows(resid * far_re, resid * far_im)))
    yield
    half_s, half_d = back[0] + back[1], back[0] - back[1]
    re, im = rows(half_s[:H], half_d[:H]), rows(half_s[H:], half_d[H:])
    even = right_dot(lanes(re[:, :H], im[:, :H]), right[2])
    odd = right_dot(lanes(re[:, H:], im[:, H:]), right[3])
    yield
    first, second = even + odd, even - odd
    back_re = lanes(first[:, :H], second[:, :H])
    back_im = lanes(first[:, H:], second[:, H:])
    unmask = lane < H - dc
    undo = lax.rem(H - dc, H)
    for p in range(2):
        if p == 0:
            update = rolled[0] * back_re + rolled[1] * back_im
            grad = patch[0] * back_re + patch[1] * back_im
        else:
            update = rolled[0] * back_im - rolled[1] * back_re
            grad = patch[0] * back_im - patch[1] * back_re
        acc[p, j0, at, :] += jnp.where(mask, update[:, :H], 0.0)
        acc[p, j0 + 2, at, :] += jnp.where(mask, 0.0, update[:, :H])
        acc[p, j0 + 1, at, :] += update[:, H:]
        a, b = turned(grad[:, :H], grad[:, H:], undo, unmask)
        pacc[p, :, :H] += a
        pacc[p, :, H:] += b
    yield


def some_windows(spots, ext, acc, probe, right, left, order, pacc, stats, rolled, patch):
    runs = [
        one_window(spot, ext, acc, probe, right, left, order, pacc, stats, rolled.at[w], patch.at[w])
        for w, spot in enumerate(spots)
    ]
    steps = 6
    for t in range(steps + LAG * (len(runs) - 1)):
        for w, run in enumerate(runs):
            if 0 <= t - LAG * w < steps:
                next(run)


def windows_kernel(pos, counts, patterns, probe, right_in, left_in, order_in, ext, acc, pacc, stats, pat, rolled, patch,
                   right, left, order, sems):
    row, col = lax.axis_index("row"), lax.axis_index("col")
    count = counts[row * 8 + col]

    def pattern_copies(s):
        return [
            pltpu.make_async_copy(patterns.at[s, :, pl.ds(k * H, H)], pat.at[s, k], sems.at[s, k]) for k in range(2)
        ]

    @pl.loop(0, count)
    def _(s):
        for copy in pattern_copies(s):
            copy.start()

    for k in range(4):
        right[k, 0], right[k, 1] = split(right_in[k])
        left[k, 0], left[k, 1] = split(left_in[k])
    order[...] = order_in[...].astype(BF16)
    for ref in (acc, pacc, stats):
        ref[...] = jnp.zeros_like(ref)

    def spot(s):
        for copy in pattern_copies(s):
            copy.wait()
        o, c = pos[0, s] - row * 512, pos[1, s] - col * 1024
        return o, c // H, c % H, pat.at[s]

    def run(spots):
        some_windows(spots, ext, acc, probe, right, left, order, pacc, stats, rolled, patch)

    @pl.loop(0, count // SIDE)
    def _(i):
        run([spot(SIDE * i + w) for w in range(SIDE)])

    @pl.loop(count // SIDE * SIDE, count)
    def _(i):
        run([spot(i)])


def windows(pos, counts, patterns, probe, tables, ext):
    vm = pl.BlockSpec(memory_space=pltpu.VMEM)
    sm = pl.BlockSpec(memory_space=pltpu.SMEM)
    hbm = pl.BlockSpec(memory_space=pl.ANY)
    return pl.pallas_call(
        windows_kernel,
        name="windows",
        out_shape=[
            jax.ShapeDtypeStruct((2, 10, 768, H), F32),
            jax.ShapeDtypeStruct((2, M, M), F32),
            jax.ShapeDtypeStruct((16, M), F32),
        ],
        in_specs=[sm, sm, hbm, vm, vm, vm, vm, vm],
        out_specs=[vm, vm, vm],
        scratch_shapes=[
            pltpu.VMEM((CAP, 2, M, H), F32),
            pltpu.VMEM((SIDE, 2, M, M), F32),
            pltpu.VMEM((SIDE, 2, M, M), F32),
            pltpu.VMEM((4, 2, M, M), BF16),
            pltpu.VMEM((4, 2, M, M), BF16),
            pltpu.VMEM((M, M), BF16),
            pltpu.SemaphoreType.DMA((CAP, 2)),
        ],
        compiler_params=pltpu.CompilerParams(vmem_limit_bytes=29 << 20),
        cost_estimate=pl.CostEstimate(flops=12 * 10**9, bytes_accessed=8 << 20, transcendentals=0),
    )(pos, counts, patterns, probe, *tables, ext)


MESH = pl.DeviceIdType.MESH
NROW, NCOL = 16, 8


def send(src, dst, ss, rs, peer):
    copy = pltpu.make_async_remote_copy(src, dst, ss, rs, device_id=peer, device_id_type=MESH)
    copy.start()
    return copy


def ring(row, step):
    return row // 4 * 4 + lax.rem(row + step + 4, 4)


def columns(k, n=1):
    return pl.ds(k * H, n * H)


def halo_kernel(sample, ext, held1, held2, ss, rs, ls):
    row, col = lax.axis_index("row"), lax.axis_index("col")
    above, below = lax.rem(row + NROW - 1, NROW), lax.rem(row + 1, NROW)
    before, after = lax.rem(col + NCOL - 1, NCOL), lax.rem(col + 1, NCOL)
    across, back = ring(above, 2), lax.rem(ring(row, 2) + 1, NROW)
    barrier = pltpu.get_barrier_semaphore()
    for peer in ((below, col), (ring(row, -1), col), (back, col), (row, after)):
        pl.semaphore_signal(barrier, inc=1, device_id=peer, device_id_type=MESH)
    pl.semaphore_wait(barrier, 4)
    number = iter(range(32))

    def go(src, dst, peer):
        n = next(number)
        return send(src, dst, ss.at[n], rs.at[n], peer)

    up = ring(row, 1), col
    top, tile, beyond = pl.ds(0, M), pl.ds(0, 512), pl.ds(512, M)

    def lower(k):
        return go(sample.at[:, top, columns(k)], ext.at[:, k, beyond], (above, col))

    hop1 = [go(sample.at[:, top, columns(2 + i)], held1.at[i], (across, col)) for i in range(2)]
    first = [lower(0), lower(1)]
    rest = [go(sample.at[:, tile, columns(k)], ext.at[:, 8 + k, tile], (row, before)) for k in range(2)]
    rest += [lower(k) for k in (4, 5, 6, 7)]
    own = [pltpu.make_async_copy(sample.at[:, tile, columns(k)], ext.at[:, k, tile], ls.at[k]) for k in range(8)]
    for copy in own:
        copy.start()
    hop1[0].wait_recv()
    hop2 = [go(held1.at[0], held2.at[0], up)]
    for k in range(2):
        first[k].wait_recv()
        rest.append(go(ext.at[:, k, beyond], ext.at[:, 8 + k, beyond], (row, before)))
    hop1[1].wait_recv()
    hop2.append(go(held1.at[1], held2.at[1], up))
    hop3 = []
    for i in range(2):
        hop2[i].wait_recv()
        hop3.append(go(held2.at[i], ext.at[:, 2 + i, beyond], up))
    for copy in first + hop1 + hop2:
        copy.wait_send()
    for copy in rest + hop3 + own:
        copy.wait()

    @pl.when(row == NROW - 1)
    def _():
        ext[:, :, 512:] = jnp.zeros_like(ext[:, :, 512:])

    @pl.when(col == NCOL - 1)
    def _():
        ext[:, 8:] = jnp.zeros_like(ext[:, 8:])


def halos(sample):
    return pl.pallas_call(
        halo_kernel,
        name="halos",
        out_shape=jax.ShapeDtypeStruct((2, 10, 768, H), F32),
        in_specs=[pl.BlockSpec(memory_space=pltpu.HBM)],
        out_specs=pl.BlockSpec(memory_space=pltpu.VMEM),
        scratch_shapes=[
            pltpu.VMEM((2, 2, M, H), F32),
            pltpu.VMEM((2, 2, M, H), F32),
            pltpu.SemaphoreType.DMA((16,)),
            pltpu.SemaphoreType.DMA((16,)),
            pltpu.SemaphoreType.DMA((8,)),
        ],
        compiler_params=pltpu.CompilerParams(collective_id=1, has_side_effects=True, vmem_limit_bytes=14 << 20),
        cost_estimate=pl.CostEstimate(flops=40 * 10**9, bytes_accessed=1 << 20, transcendentals=0),
    )(sample)


def tail_kernel(counts, pacc, stats, acc, out, coeff, misfit, down, came, mine1, got1, mine2, got2, part, wide,
                turn, low, held1, held2, s1, r1, s2, r2, s3, r3, s4, r4, ss, rs, ls):
    row, col = lax.axis_index("row"), lax.axis_index("col")

    def col_peer(k):
        return row, lax.rem(col + k, NCOL)

    def row_peer(k):
        return lax.rem(row + k, NROW), col

    barrier = pltpu.get_barrier_semaphore()
    for k in range(1, NCOL):
        pl.semaphore_signal(barrier, inc=1, device_id=col_peer(k), device_id_type=MESH)
    for k in range(1, NROW):
        pl.semaphore_signal(barrier, inc=1, device_id=row_peer(k), device_id_type=MESH)
    beyond, tile, edge = pl.ds(512, M), pl.ds(0, 512), pl.ds(8, 2)
    own = pltpu.make_async_copy(acc.at[:, pl.ds(0, 2), beyond], turn, ls)
    own.start()
    for p in range(2):
        for b in range(2):
            for h in range(2):
                piece = 4 * p + 2 * b + h
                mine1[piece, :H] = pacc[p, h * H : (h + 1) * H, b * H : (b + 1) * H]
                mine1[piece, H:] = stats[:, :H] + stats[:, H:]
    pl.semaphore_wait(barrier, NCOL + NROW - 2)
    number = iter(range(32))

    def go(src, dst, peer):
        n = next(number)
        return send(src, dst, ss.at[n], rs.at[n], peer)

    def lower(k):
        return go(acc.at[:, k, beyond], down.at[:, k], row_peer(1))

    across, back = (ring(lax.rem(row + 1, NROW), 2), col), (ring(row, -1), col)
    hop1 = [go(acc.at[:, 2 + i, beyond], held1.at[i], across) for i in range(2)]
    rest = [lower(7), lower(6), lower(5)]
    copies = [
        send(mine1.at[lax.rem(col + k, NCOL)], got1.at[k - 1], s1.at[k - 1], r1.at[k - 1], col_peer(k))
        for k in range(1, NCOL)
    ]
    hop1[0].wait_recv()
    hop2 = [go(held1.at[0], held2.at[0], back)]
    for copy in copies:
        copy.wait()
    total = mine1[col]
    for k in range(NCOL - 1):
        total = total + got1[k]
    for k in range(NROW):
        mine2[k, :8] = total[8 * k : 8 * k + 8]
        mine2[k, 8:] = total[H:]
    copies = [
        send(mine2.at[lax.rem(row + k, NROW)], got2.at[k - 1], s2.at[k - 1], r2.at[k - 1], row_peer(k))
        for k in range(1, NROW)
    ]
    corner = go(acc.at[:, edge, beyond], low, col_peer(1))
    rest.append(lower(4))
    hop1[1].wait_recv()
    hop2.append(go(held1.at[1], held2.at[1], back))
    rest.append(go(acc.at[:, edge, tile], came, col_peer(1)))
    for copy in copies:
        copy.wait()
    total = mine2[row]
    for k in range(NROW - 1):
        total = total + got2[k]
    visits = jnp.sum(counts[...].astype(F32))
    pixels = M * M * visits
    mean = jnp.full((8, H), jnp.sum(total[16:])) / pixels
    factor = 4.0 / (mean * mean)
    coeff[...] = factor
    misfit[...] = jnp.full((8, H), jnp.sum(total[8:16])) / (mean * mean * pixels)
    part[row] = total[:8] * (factor / visits)
    copies = [send(part.at[row], part.at[row], s3.at[k - 1], r3.at[k - 1], row_peer(k)) for k in range(1, NROW)]
    hop2[0].wait_recv()
    hop3 = [go(held2.at[0], down.at[:, 2], back)]
    own.wait()
    corner.wait_recv()
    turn[...] += jnp.where(col > 0, low[...], 0.0)
    rest.append(go(turn, down.at[:, pl.ds(0, 2)], row_peer(1)))
    for copy in copies:
        copy.wait()
    copies = [send(part, wide.at[col], s4.at[k - 1], r4.at[k - 1], col_peer(k)) for k in range(1, NCOL)]
    wide[col] = part[...]
    hop2[1].wait_recv()
    hop3.append(go(held2.at[1], down.at[:, 3], back))
    for copy in copies:
        copy.wait()
    for p in range(2):
        for b in range(2):
            for h in range(2):
                out[p, h * H : (h + 1) * H, b * H : (b + 1) * H] = wide[4 * p + 2 * b + h].reshape(H, H)
    for copy in [corner] + hop1 + hop2:
        copy.wait_send()
    for copy in rest + hop3:
        copy.wait()


def tail(counts, pacc, stats, acc):
    vm = pl.BlockSpec(memory_space=pltpu.VMEM)
    sm = pl.BlockSpec(memory_space=pltpu.SMEM)
    hbm = pl.BlockSpec(memory_space=pl.ANY)
    numbers = (NCOL - 1, NCOL - 1, NROW - 1, NROW - 1, NROW - 1, NROW - 1, NCOL - 1, NCOL - 1, 13, 13)
    tile = jax.ShapeDtypeStruct((8, H), F32)
    return pl.pallas_call(
        tail_kernel,
        name="tail",
        out_shape=[
            jax.ShapeDtypeStruct((2, M, M), F32), tile, tile,
            jax.ShapeDtypeStruct((2, 8, M, H), F32), jax.ShapeDtypeStruct((2, 2, 512, H), F32),
        ],
        in_specs=[vm, vm, vm, hbm],
        out_specs=[vm, vm, vm, hbm, hbm],
        scratch_shapes=[
            pltpu.VMEM((NCOL, H + 16, H), F32),
            pltpu.VMEM((NCOL - 1, H + 16, H), F32),
            pltpu.VMEM((NROW, 24, H), F32),
            pltpu.VMEM((NROW - 1, 24, H), F32),
            pltpu.VMEM((NROW, 8, H), F32),
            pltpu.VMEM((NCOL, NROW, 8, H), F32),
            pltpu.VMEM((2, 2, M, H), F32),
            pltpu.VMEM((2, 2, M, H), F32),
            pltpu.VMEM((2, 2, M, H), F32),
            pltpu.VMEM((2, 2, M, H), F32),
        ]
        + [pltpu.SemaphoreType.DMA((n,)) for n in numbers]
        + [pltpu.SemaphoreType.DMA],
        compiler_params=pltpu.CompilerParams(collective_id=0, has_side_effects=True, vmem_limit_bytes=14 << 20),
        cost_estimate=pl.CostEstimate(flops=40 * 10**9, bytes_accessed=1 << 20, transcendentals=0),
    )(counts, pacc, stats, acc)


def finish_kernel(coeff, misfit, probe, acc, came, down, out, probe_out, misfit_out, tile, sems):
    row, col = lax.axis_index("row"), lax.axis_index("col")
    factor = coeff[0:1, 0:1]
    ends = []
    for k in (2, 3, 4, 5, 6, 7, 0, 1):
        upper, lower = acc[:, k, :M] + jnp.where(row > 0, down[:, k], 0.0), acc[:, k, M:512]
        if k < 2:
            upper = upper + jnp.where(col > 0, came[:, k, :M], 0.0)
            lower = lower + jnp.where(col > 0, came[:, k, M:], 0.0)
        tile[k, :, :M] = upper * factor
        tile[k, :, M:] = lower * factor
        ends.append(pltpu.make_async_copy(tile.at[k], out.at[:, :, columns(k)], sems.at[k]))
        ends[-1].start()
    probe_out[...] = probe[...]
    misfit_out[...] = misfit[0:1, 0:1]
    for copy in ends:
        copy.wait()


def finished(coeff, misfit, probe, acc, came, down):
    vm = pl.BlockSpec(memory_space=pltpu.VMEM)
    return pl.pallas_call(
        finish_kernel,
        name="finished",
        out_shape=[
            jax.ShapeDtypeStruct((2, 512, 1024), F32),
            jax.ShapeDtypeStruct((2, M, M), F32),
            jax.ShapeDtypeStruct((1, 1), F32),
        ],
        in_specs=[vm] * 6,
        out_specs=[pl.BlockSpec(memory_space=pl.ANY), vm, vm],
        scratch_shapes=[pltpu.VMEM((8, 2, 512, H), F32), pltpu.SemaphoreType.DMA((8,))],
        compiler_params=pltpu.CompilerParams(vmem_limit_bytes=28 << 20),
        cost_estimate=pl.CostEstimate(flops=10**7, bytes_accessed=10 << 20, transcendentals=0),
    )(coeff, misfit, probe, acc, came, down)


def body(sample, probe, patterns, positions, counts):
    tables = tuple(jnp.asarray(t) for t in dft_tables())
    ext = halos(pltpu.with_memory_space_constraint(sample, pltpu.HBM))
    acc, pacc, stats = windows(positions.T, counts, patterns, probe, tables, ext)
    probe_sum, coeff, misfit, down, came = tail(counts.reshape(1, H), pacc, stats, acc)
    object_grad, probe_grad, mean_misfit = finished(coeff, misfit, probe_sum, acc, came, down)
    return object_grad, probe_grad, mean_misfit.reshape(())


def solution(mesh):
    in_specs = (
        P(None, "row", "col"),
        P(),
        P(("row", "col"), None, None),
        P(("row", "col"), None),
        P(),
    )
    out_specs = (P(None, "row", "col"), P(), P())
    return jax.shard_map(body, mesh=mesh, in_specs=in_specs, out_specs=out_specs, check_vma=False)
```

```python
import math

import jax
import jax.numpy as jnp
import numpy as np
from jax import lax
from jax.experimental import pallas as pl
from jax.experimental.pallas import tpu as pltpu
from jax.sharding import PartitionSpec as P

F32 = jnp.float32
BF16 = jnp.bfloat16
M = 256
H = 128
CAP = 16
SIDE = 2
LAG = 0


def dft_tables():
    n = np.arange(H)[:, None]
    m = np.arange(H)[None, :]
    right, left = [], []
    for sign in (-1.0, 1.0):
        for odd in (0, 1):
            if sign < 0:
                angle = 2 * math.pi * (n * (2 * m + odd) % M) / M
            else:
                angle = 2 * math.pi * ((2 * n + odd) * m % M) / M
            re, im = np.cos(angle) / 16.0, sign * np.sin(angle) / 16.0
            right.append(np.block([[re, im], [-im, re]]))
            left.append(right[-1].T)
    order = np.zeros((M, M), np.float32)
    k = np.arange(M)
    order[k, k // 2 + H * (k % 2)] = 1.0
    return np.stack(right).astype(np.float32), np.stack(left).astype(np.float32), order


def split(value):
    high = value.astype(BF16)
    return high, (value - high.astype(F32)).astype(BF16)


def dot(a, b):
    return jnp.dot(a, b, preferred_element_type=F32)


def right_dot(value, table):
    high, low = split(value)
    return dot(high, table[0]) + dot(low, table[0]) + dot(high, table[1])


def left_dot(table, value):
    high, low = split(value)
    both = dot(table.reshape(2 * M, M), high)
    return both[:M] + both[M:] + dot(table[0], low)


def lanes(a, b):
    return jnp.concatenate([a, b], axis=1)


def rows(*parts):
    return jnp.concatenate(parts, axis=0)


def one_window(spot, ext, acc, probe, right, left, order, pacc, stats, rolled, patch):
    top, j0, dc, pat = spot
    lane = lax.broadcasted_iota(jnp.int32, (M, H), 1)
    mask = lane >= dc
    at = pl.ds(top, M)

    def turned(a, b, shift, keep):
        a, b = pltpu.roll(a, shift, 1), pltpu.roll(b, shift, 1)
        return jnp.where(keep, a, b), jnp.where(keep, b, a)

    for p in range(2):
        a, b = turned(probe[p, :, :H], probe[p, :, H:], dc, mask)
        rolled[p, :, :H] = a
        rolled[p, :, H:] = b
        patch[p, :, :H] = jnp.where(mask, ext[p, j0, at, :], ext[p, j0 + 2, at, :])
        patch[p, :, H:] = ext[p, j0 + 1, at, :]
    wave_re = rolled[0] * patch[0] - rolled[1] * patch[1]
    wave_im = rolled[0] * patch[1] + rolled[1] * patch[0]
    sums = lanes(wave_re[:, :H] + wave_re[:, H:], wave_im[:, :H] + wave_im[:, H:])
    difs = lanes(wave_re[:, :H] - wave_re[:, H:], wave_im[:, :H] - wave_im[:, H:])
    yield
    even = right_dot(sums, right[0])
    odd = right_dot(difs, right[1])
    yield
    halves = ((even[:H] + even[H:], odd[:H] + odd[H:]), (even[:H] - even[H:], odd[:H] - odd[H:]))
    fars = []
    evens, odds = pl.ds(0, H, 2), pl.ds(1, H, 2)
    level = rows(lanes(pat[0, evens, :], pat[1, evens, :]), lanes(pat[0, odds, :], pat[1, odds, :]))
    stats[8:] += jnp.sum(level.reshape(32, 8, M), axis=0)
    high, low = split(level)
    level = dot(high, order[...]) + dot(low, order[...])
    levels = [level[:H], level[H:]]
    for parity, (e, o) in enumerate(halves):
        fars.append(left_dot(left[parity], rows(lanes(e[:, :H], o[:, :H]), lanes(e[:, H:], o[:, H:]))))
    yield
    back = []
    for parity, far in enumerate(fars):
        far_re, far_im = far[:H], far[H:]
        resid = far_re * far_re + far_im * far_im - levels[parity]
        stats[:8] += jnp.sum((resid * resid).reshape(16, 8, M), axis=0)
        back.append(left_dot(left[2 + parity], rows(resid * far_re, resid * far_im)))
    yield
    half_s, half_d = back[0] + back[1], back[0] - back[1]
    re, im = rows(half_s[:H], half_d[:H]), rows(half_s[H:], half_d[H:])
    even = right_dot(lanes(re[:, :H], im[:, :H]), right[2])
    odd = right_dot(lanes(re[:, H:], im[:, H:]), right[3])
    yield
    first, second = even + odd, even - odd
    back_re = lanes(first[:, :H], second[:, :H])
    back_im = lanes(first[:, H:], second[:, H:])
    unmask = lane < H - dc
    undo = lax.rem(H - dc, H)
    for p in range(2):
        if p == 0:
            update = rolled[0] * back_re + rolled[1] * back_im
            grad = patch[0] * back_re + patch[1] * back_im
        else:
            update = rolled[0] * back_im - rolled[1] * back_re
            grad = patch[0] * back_im - patch[1] * back_re
        acc[p, j0, at, :] += jnp.where(mask, update[:, :H], 0.0)
        acc[p, j0 + 2, at, :] += jnp.where(mask, 0.0, update[:, :H])
        acc[p, j0 + 1, at, :] += update[:, H:]
        a, b = turned(grad[:, :H], grad[:, H:], undo, unmask)
        pacc[p, :, :H] += a
        pacc[p, :, H:] += b
    yield


def some_windows(spots, ext, acc, probe, right, left, order, pacc, stats, rolled, patch):
    runs = [
        one_window(spot, ext, acc, probe, right, left, order, pacc, stats, rolled.at[w], patch.at[w])
        for w, spot in enumerate(spots)
    ]
    steps = 6
    for t in range(steps + LAG * (len(runs) - 1)):
        for w, run in enumerate(runs):
            if 0 <= t - LAG * w < steps:
                next(run)


def windows_kernel(pos, counts, patterns, probe, right_in, left_in, order_in, ext, acc, pacc, stats, pat, rolled, patch,
                   right, left, order, sems):
    row, col = lax.axis_index("row"), lax.axis_index("col")
    count = counts[row * 8 + col]

    def pattern_copies(s):
        return [
            pltpu.make_async_copy(patterns.at[s, :, pl.ds(k * H, H)], pat.at[s, k], sems.at[s, k]) for k in range(2)
        ]

    @pl.loop(0, count)
    def _(s):
        for copy in pattern_copies(s):
            copy.start()

    for k in range(4):
        right[k, 0], right[k, 1] = split(right_in[k])
        left[k, 0], left[k, 1] = split(left_in[k])
    order[...] = order_in[...].astype(BF16)
    for ref in (acc, pacc, stats):
        ref[...] = jnp.zeros_like(ref)

    def spot(s):
        for copy in pattern_copies(s):
            copy.wait()
        o, c = pos[0, s] - row * 512, pos[1, s] - col * 1024
        return o, c // H, c % H, pat.at[s]

    def run(spots):
        some_windows(spots, ext, acc, probe, right, left, order, pacc, stats, rolled, patch)

    @pl.loop(0, count // SIDE)
    def _(i):
        run([spot(SIDE * i + w) for w in range(SIDE)])

    @pl.loop(count // SIDE * SIDE, count)
    def _(i):
        run([spot(i)])


def windows(pos, counts, patterns, probe, tables, ext):
    vm = pl.BlockSpec(memory_space=pltpu.VMEM)
    sm = pl.BlockSpec(memory_space=pltpu.SMEM)
    hbm = pl.BlockSpec(memory_space=pl.ANY)
    return pl.pallas_call(
        windows_kernel,
        name="windows",
        out_shape=[
            jax.ShapeDtypeStruct((2, 10, 768, H), F32),
            jax.ShapeDtypeStruct((2, M, M), F32),
            jax.ShapeDtypeStruct((16, M), F32),
        ],
        in_specs=[sm, sm, hbm, vm, vm, vm, vm, vm],
        out_specs=[vm, vm, vm],
        scratch_shapes=[
            pltpu.VMEM((CAP, 2, M, H), F32),
            pltpu.VMEM((SIDE, 2, M, M), F32),
            pltpu.VMEM((SIDE, 2, M, M), F32),
            pltpu.VMEM((4, 2, M, M), BF16),
            pltpu.VMEM((4, 2, M, M), BF16),
            pltpu.VMEM((M, M), BF16),
            pltpu.SemaphoreType.DMA((CAP, 2)),
        ],
        compiler_params=pltpu.CompilerParams(vmem_limit_bytes=29 << 20),
        cost_estimate=pl.CostEstimate(flops=12 * 10**9, bytes_accessed=8 << 20, transcendentals=0),
    )(pos, counts, patterns, probe, *tables, ext)


MESH = pl.DeviceIdType.MESH
NROW, NCOL = 16, 8


def send(src, dst, ss, rs, peer):
    copy = pltpu.make_async_remote_copy(src, dst, ss, rs, device_id=peer, device_id_type=MESH)
    copy.start()
    return copy


def ring(row, step):
    return row // 4 * 4 + lax.rem(row + step + 4, 4)


def columns(k, n=1):
    return pl.ds(k * H, n * H)


def halo_kernel(sample, ext, held1, held2, ss, rs, ls):
    row, col = lax.axis_index("row"), lax.axis_index("col")
    above, below = lax.rem(row + NROW - 1, NROW), lax.rem(row + 1, NROW)
    before, after = lax.rem(col + NCOL - 1, NCOL), lax.rem(col + 1, NCOL)
    across, back = ring(above, 2), lax.rem(ring(row, 2) + 1, NROW)
    barrier = pltpu.get_barrier_semaphore()
    for peer in ((below, col), (ring(row, -1), col), (back, col), (row, after)):
        pl.semaphore_signal(barrier, inc=1, device_id=peer, device_id_type=MESH)
    pl.semaphore_wait(barrier, 4)
    number = iter(range(32))

    def go(src, dst, peer):
        n = next(number)
        return send(src, dst, ss.at[n], rs.at[n], peer)

    up = ring(row, 1), col
    top, tile, beyond = pl.ds(0, M), pl.ds(0, 512), pl.ds(512, M)

    def lower(k):
        return go(sample.at[:, top, columns(k)], ext.at[:, k, beyond], (above, col))

    hop1 = [go(sample.at[:, top, columns(2 + i)], held1.at[i], (across, col)) for i in range(2)]
    first = [lower(0), lower(1)]
    rest = [go(sample.at[:, tile, columns(k)], ext.at[:, 8 + k, tile], (row, before)) for k in range(2)]
    rest += [lower(k) for k in (4, 5, 6, 7)]
    own = [pltpu.make_async_copy(sample.at[:, tile, columns(k)], ext.at[:, k, tile], ls.at[k]) for k in range(8)]
    for copy in own:
        copy.start()
    hop1[0].wait_recv()
    hop2 = [go(held1.at[0], held2.at[0], up)]
    for k in range(2):
        first[k].wait_recv()
        rest.append(go(ext.at[:, k, beyond], ext.at[:, 8 + k, beyond], (row, before)))
    hop1[1].wait_recv()
    hop2.append(go(held1.at[1], held2.at[1], up))
    hop3 = []
    for i in range(2):
        hop2[i].wait_recv()
        hop3.append(go(held2.at[i], ext.at[:, 2 + i, beyond], up))
    for copy in first + hop1 + hop2:
        copy.wait_send()
    for copy in rest + hop3 + own:
        copy.wait()

    @pl.when(row == NROW - 1)
    def _():
        ext[:, :, 512:] = jnp.zeros_like(ext[:, :, 512:])

    @pl.when(col == NCOL - 1)
    def _():
        ext[:, 8:] = jnp.zeros_like(ext[:, 8:])


def halos(sample):
    return pl.pallas_call(
        halo_kernel,
        name="halos",
        out_shape=jax.ShapeDtypeStruct((2, 10, 768, H), F32),
        in_specs=[pl.BlockSpec(memory_space=pltpu.HBM)],
        out_specs=pl.BlockSpec(memory_space=pltpu.VMEM),
        scratch_shapes=[
            pltpu.VMEM((2, 2, M, H), F32),
            pltpu.VMEM((2, 2, M, H), F32),
            pltpu.SemaphoreType.DMA((16,)),
            pltpu.SemaphoreType.DMA((16,)),
            pltpu.SemaphoreType.DMA((8,)),
        ],
        compiler_params=pltpu.CompilerParams(collective_id=1, has_side_effects=True, vmem_limit_bytes=14 << 20),
        cost_estimate=pl.CostEstimate(flops=40 * 10**9, bytes_accessed=1 << 20, transcendentals=0),
    )(sample)


def tail_kernel(counts, pacc, stats, acc, out, coeff, misfit, down, came, mine1, got1, mine2, got2, part, wide,
                turn, low, held1, held2, s1, r1, s2, r2, s3, r3, s4, r4, ss, rs, ls):
    row, col = lax.axis_index("row"), lax.axis_index("col")

    def col_peer(k):
        return row, lax.rem(col + k, NCOL)

    def row_peer(k):
        return lax.rem(row + k, NROW), col

    barrier = pltpu.get_barrier_semaphore()
    for k in range(1, NCOL):
        pl.semaphore_signal(barrier, inc=1, device_id=col_peer(k), device_id_type=MESH)
    for k in range(1, NROW):
        pl.semaphore_signal(barrier, inc=1, device_id=row_peer(k), device_id_type=MESH)
    beyond, tile, edge = pl.ds(512, M), pl.ds(0, 512), pl.ds(8, 2)
    own = pltpu.make_async_copy(acc.at[:, pl.ds(0, 2), beyond], turn, ls)
    own.start()
    both = stats[:, :H] + stats[:, H:]
    at = lax.broadcasted_iota(jnp.int32, (8, H), 0)
    missed, seen = jnp.sum(both[:8], axis=0, keepdims=True), jnp.sum(both[8:], axis=0, keepdims=True)
    sums = jnp.where(at == 0, missed, jnp.where(at == 1, seen, 0.0))
    for p in range(2):
        for b in range(2):
            for h in range(2):
                piece = 4 * p + 2 * b + h
                mine1[piece, :H] = pacc[p, h * H : (h + 1) * H, b * H : (b + 1) * H]
                mine1[piece, H:] = sums
    pl.semaphore_wait(barrier, NCOL + NROW - 2)
    number = iter(range(32))

    def go(src, dst, peer):
        n = next(number)
        return send(src, dst, ss.at[n], rs.at[n], peer)

    def lower(k):
        return go(acc.at[:, k, beyond], down.at[:, k], row_peer(1))

    across, back = (ring(lax.rem(row + 1, NROW), 2), col), (ring(row, -1), col)
    hop1 = [go(acc.at[:, 2 + i, beyond], held1.at[i], across) for i in range(2)]
    rest = [lower(7), lower(6), lower(5)]
    copies = [
        send(mine1.at[lax.rem(col + k, NCOL)], got1.at[k - 1], s1.at[k - 1], r1.at[k - 1], col_peer(k))
        for k in range(1, NCOL)
    ]
    hop1[0].wait_recv()
    hop2 = [go(held1.at[0], held2.at[0], back)]
    for copy in copies:
        copy.wait()
    total = mine1[col]
    for k in range(NCOL - 1):
        total = total + got1[k]
    for k in range(NROW):
        mine2[k, :8] = total[8 * k : 8 * k + 8]
        mine2[k, 8:] = total[H:]
    copies = [
        send(mine2.at[lax.rem(row + k, NROW)], got2.at[k - 1], s2.at[k - 1], r2.at[k - 1], row_peer(k))
        for k in range(1, NROW)
    ]
    corner = go(acc.at[:, edge, beyond], low, col_peer(1))
    rest.append(lower(4))
    hop1[1].wait_recv()
    hop2.append(go(held1.at[1], held2.at[1], back))
    rest.append(go(acc.at[:, edge, tile], came, col_peer(1)))
    for copy in copies:
        copy.wait()
    total = mine2[row]
    for k in range(NROW - 1):
        total = total + got2[k]
    visits = jnp.sum(counts[...].astype(F32))
    pixels = M * M * visits
    mean = jnp.full((8, H), jnp.sum(total[9:10])) / pixels
    factor = 4.0 / (mean * mean)
    coeff[...] = factor
    misfit[...] = jnp.full((8, H), jnp.sum(total[8:9])) / (mean * mean * pixels)
    part[row] = total[:8] * (factor / visits)
    copies = [send(part.at[row], part.at[row], s3.at[k - 1], r3.at[k - 1], row_peer(k)) for k in range(1, NROW)]
    own.wait()
    corner.wait_recv()
    turn[...] += jnp.where(col > 0, low[...], 0.0)
    rest.append(go(turn, down.at[:, pl.ds(0, 2)], row_peer(1)))
    hop2[0].wait_recv()
    hop3 = [go(held2.at[0], down.at[:, 2], back)]
    for copy in copies:
        copy.wait()
    copies = [send(part, wide.at[col], s4.at[k - 1], r4.at[k - 1], col_peer(k)) for k in range(1, NCOL)]
    wide[col] = part[...]
    hop2[1].wait_recv()
    hop3.append(go(held2.at[1], down.at[:, 3], back))
    for copy in copies:
        copy.wait()
    for p in range(2):
        for b in range(2):
            for h in range(2):
                out[p, h * H : (h + 1) * H, b * H : (b + 1) * H] = wide[4 * p + 2 * b + h].reshape(H, H)
    for copy in [corner] + hop1 + hop2:
        copy.wait_send()
    for copy in rest + hop3:
        copy.wait()


def tail(counts, pacc, stats, acc):
    vm = pl.BlockSpec(memory_space=pltpu.VMEM)
    sm = pl.BlockSpec(memory_space=pltpu.SMEM)
    hbm = pl.BlockSpec(memory_space=pl.ANY)
    numbers = (NCOL - 1, NCOL - 1, NROW - 1, NROW - 1, NROW - 1, NROW - 1, NCOL - 1, NCOL - 1, 13, 13)
    tile = jax.ShapeDtypeStruct((8, H), F32)
    return pl.pallas_call(
        tail_kernel,
        name="tail",
        out_shape=[
            jax.ShapeDtypeStruct((2, M, M), F32), tile, tile,
            jax.ShapeDtypeStruct((2, 8, M, H), F32), jax.ShapeDtypeStruct((2, 2, 512, H), F32),
        ],
        in_specs=[vm, vm, vm, hbm],
        out_specs=[vm, vm, vm, hbm, hbm],
        scratch_shapes=[
            pltpu.VMEM((NCOL, H + 8, H), F32),
            pltpu.VMEM((NCOL - 1, H + 8, H), F32),
            pltpu.VMEM((NROW, 16, H), F32),
            pltpu.VMEM((NROW - 1, 16, H), F32),
            pltpu.VMEM((NROW, 8, H), F32),
            pltpu.VMEM((NCOL, NROW, 8, H), F32),
            pltpu.VMEM((2, 2, M, H), F32),
            pltpu.VMEM((2, 2, M, H), F32),
            pltpu.VMEM((2, 2, M, H), F32),
            pltpu.VMEM((2, 2, M, H), F32),
        ]
        + [pltpu.SemaphoreType.DMA((n,)) for n in numbers]
        + [pltpu.SemaphoreType.DMA],
        compiler_params=pltpu.CompilerParams(collective_id=0, has_side_effects=True, vmem_limit_bytes=14 << 20),
        cost_estimate=pl.CostEstimate(flops=40 * 10**9, bytes_accessed=1 << 20, transcendentals=0),
    )(counts, pacc, stats, acc)


def finish_kernel(coeff, misfit, probe, acc, came, down, out, probe_out, misfit_out, tile, sems):
    row, col = lax.axis_index("row"), lax.axis_index("col")
    factor = coeff[0:1, 0:1]
    ends = []
    for k in (2, 3, 4, 5, 6, 7, 0, 1):
        upper, lower = acc[:, k, :M] + jnp.where(row > 0, down[:, k], 0.0), acc[:, k, M:512]
        if k < 2:
            upper = upper + jnp.where(col > 0, came[:, k, :M], 0.0)
            lower = lower + jnp.where(col > 0, came[:, k, M:], 0.0)
        tile[k, :, :M] = upper * factor
        tile[k, :, M:] = lower * factor
        ends.append(pltpu.make_async_copy(tile.at[k], out.at[:, :, columns(k)], sems.at[k]))
        ends[-1].start()
    probe_out[...] = probe[...]
    misfit_out[...] = misfit[0:1, 0:1]
    for copy in ends:
        copy.wait()


def finished(coeff, misfit, probe, acc, came, down):
    vm = pl.BlockSpec(memory_space=pltpu.VMEM)
    return pl.pallas_call(
        finish_kernel,
        name="finished",
        out_shape=[
            jax.ShapeDtypeStruct((2, 512, 1024), F32),
            jax.ShapeDtypeStruct((2, M, M), F32),
            jax.ShapeDtypeStruct((1, 1), F32),
        ],
        in_specs=[vm] * 6,
        out_specs=[pl.BlockSpec(memory_space=pl.ANY), vm, vm],
        scratch_shapes=[pltpu.VMEM((8, 2, 512, H), F32), pltpu.SemaphoreType.DMA((8,))],
        compiler_params=pltpu.CompilerParams(vmem_limit_bytes=28 << 20),
        cost_estimate=pl.CostEstimate(flops=10**7, bytes_accessed=10 << 20, transcendentals=0),
    )(coeff, misfit, probe, acc, came, down)


def body(sample, probe, patterns, positions, counts):
    tables = tuple(jnp.asarray(t) for t in dft_tables())
    ext = halos(pltpu.with_memory_space_constraint(sample, pltpu.HBM))
    acc, pacc, stats = windows(positions.T, counts, patterns, probe, tables, ext)
    probe_sum, coeff, misfit, down, came = tail(counts.reshape(1, H), pacc, stats, acc)
    object_grad, probe_grad, mean_misfit = finished(coeff, misfit, probe_sum, acc, came, down)
    return object_grad, probe_grad, mean_misfit.reshape(())


def solution(mesh):
    in_specs = (
        P(None, "row", "col"),
        P(),
        P(("row", "col"), None, None),
        P(("row", "col"), None),
        P(),
    )
    out_specs = (P(None, "row", "col"), P(), P())
    return jax.shard_map(body, mesh=mesh, in_specs=in_specs, out_specs=out_specs, check_vma=False)
```
